32 devices in a mesh: replica: 16 (over z, y, x), shard: 2 (over core).
Axes of the slice: x: 2, y: 2, z: 4, core: 2. Of those that a mesh axis runs over, the one named last changes fastest.
Arguments:
- images: bfloat16 [256, 14, 14, 512], P(('replica', 'shard')), may hold values from -6 to 6
- out_grad: bfloat16 [256, 14, 14, 512], P(('replica', 'shard')), may hold values from -6 to 6
- image_counts: int32 [32], P(('replica', 'shard')), may hold values from 4 to 8, as said below
- regions: int32 [196], replicated, may hold values from 0 to 8, as said below
- relative_index: int32 [49, 49], replicated, may hold values from 0 to 168, as said below
- norm1_gain: bfloat16 [512], P('shard'), may hold values from 0.5 to 1.5
- norm1_bias: bfloat16 [512], P('shard'), may hold values from -3 to 3
- qkv_weight: bfloat16 [512, 1536], P('shard'), may hold values from -0.25 to 0.25
- query_bias: bfloat16 [512], P('shard'), may hold values from -3 to 3
- value_bias: bfloat16 [512], P('shard'), may hold values from -3 to 3
- bias_table: bfloat16 [169, 16], P(None, 'shard'), may hold values from -4 to 4
- proj_weight: bfloat16 [512, 512], P('shard'), may hold values from -0.75 to 0.75
- proj_bias: bfloat16 [512], P('shard'), may hold values from -3 to 3
- norm2_gain: bfloat16 [512], P('shard'), may hold values from 0.5 to 1.5
- norm2_bias: bfloat16 [512], P('shard'), may hold values from -3 to 3
- fc1_weight: bfloat16 [512, 2048], P('shard'), may hold values from -0.25 to 0.25
- fc1_bias: bfloat16 [2048], P('shard'), may hold values from -3 to 3
- fc2_weight: bfloat16 [2048, 512], P('shard'), may hold values from -0.1875 to 0.1875
- fc2_bias: bfloat16 [512], P('shard'), may hold values from -3 to 3
Outputs:
- output: bfloat16 [256, 14, 14, 512], P(('replica', 'shard'))
- grad_images: bfloat16 [256, 14, 14, 512], P(('replica', 'shard'))
- grad_norm1_gain: float32 [512], P('shard')
- grad_norm1_bias: float32 [512], P('shard')
- grad_qkv_weight: float32 [512, 1536], P('shard')
- grad_query_bias: float32 [512], P('shard')
- grad_value_bias: float32 [512], P('shard')
- grad_bias_table: float32 [169, 16], P(None, 'shard')
- grad_proj_weight: float32 [512, 512], P('shard')
- grad_proj_bias: float32 [512], P('shard')
- grad_norm2_gain: float32 [512], P('shard')
- grad_norm2_bias: float32 [512], P('shard')
- grad_fc1_weight: float32 [512, 2048], P('shard')
- grad_fc1_bias: float32 [2048], P('shard')
- grad_fc2_weight: float32 [2048, 512], P('shard')
- grad_fc2_bias: float32 [512], P('shard')
The draws below stay inside these ranges and needn't reach their ends.
Inputs may be any that keep to these rules, and one draw needn't show every extreme that they name: Each device holds 8 image slots; its first image_counts slots are live, the others are left out of every gradient. Some device is full. `regions`: label 3 times the band of rows plus the band of columns of each position of the shifted grid, bands cut at two places along each dimension; two tokens of a window attend to each other only where their labels agree. `relative_index`: pairs of window positions with the same offset share an entry, and every entry is used.
All inputs are finite; a program needn't handle non-finite values.
Results may differ from the reference program's by a relative error of at most 0.013.
Values may be sent and summed in bfloat16 or wider, within the bound.
No kernel may reach another device: no remote copies, remote signals or barrier semaphores. Data moves between devices by JAX's collectives and lax.ppermute only.
A program may use at most 192 MiB of HBM per device.

```python
import jax
import jax.numpy as jnp
from jax import lax

D = 512
HEADS = 16
HEAD = 32
FF = 2048
SIDE = 14
WIN = 7
SHIFT = 3
IMG_CAP = 8
TABLE = 169
HOLDERS = 32
IMAGES = 256


def draw_image_counts(key, part):
    key = jax.random.fold_in(key, 11)
    first_key, pick_key = jax.random.split(key)
    least = max(1, IMG_CAP // 2)
    counts = jax.random.randint(first_key, (HOLDERS,), least, IMG_CAP + 1, dtype=jnp.int32)
    chosen = jax.random.randint(pick_key, (), 0, HOLDERS, dtype=jnp.int32)
    return jnp.where(jnp.arange(HOLDERS, dtype=jnp.int32) == chosen, IMG_CAP, counts).astype(jnp.int32)


def draw_regions(key, part):
    key = jax.random.fold_in(key, 23)
    keyset = jax.random.split(key, 4)
    half = SIDE // 2
    row_first = jax.random.randint(keyset[0], (), 1, half + 1, dtype=jnp.int32)
    row_second = jax.random.randint(keyset[1], (), half + 1, SIDE, dtype=jnp.int32)
    col_first = jax.random.randint(keyset[2], (), 1, half + 1, dtype=jnp.int32)
    col_second = jax.random.randint(keyset[3], (), half + 1, SIDE, dtype=jnp.int32)
    place = jnp.arange(SIDE, dtype=jnp.int32)
    row_band = (place >= row_first).astype(jnp.int32) + (place >= row_second).astype(jnp.int32)
    col_band = (place >= col_first).astype(jnp.int32) + (place >= col_second).astype(jnp.int32)
    return (row_band[:, None] * 3 + col_band[None, :]).reshape(SIDE * SIDE).astype(jnp.int32)


def draw_relative_index(key, part):
    key = jax.random.fold_in(key, 37)
    order = jax.random.permutation(key, TABLE).astype(jnp.int32)
    place = jnp.arange(WIN * WIN, dtype=jnp.int32)
    row_pos = place // WIN
    col_pos = place % WIN
    base = (row_pos[:, None] - row_pos[None, :] + WIN - 1) * (2 * WIN - 1) + (col_pos[:, None] - col_pos[None, :] + WIN - 1)
    return order[base].astype(jnp.int32)


def block_levels(stream_key, dims, cuts, smallest, high):
    def one(dim, parts):
        steps = jax.random.uniform(jax.random.fold_in(jax.random.fold_in(stream_key, 6), dim), (parts,), jnp.float32, smallest / len(cuts), high / len(cuts))
        return jnp.repeat(jnp.exp(steps), dims[dim] // parts).reshape((-1,) + (1,) * (len(dims) - dim - 1))

    level = one(*cuts[0])
    for cut in cuts[1:]:
        level = level * one(*cut)
    return level


def noise(own_key, dims, scale, bound, cuts=(), kind=jnp.bfloat16):
    entries = jax.random.normal(own_key, dims, jnp.float32) * scale
    if len(cuts) > 0:
        entries = block_levels(own_key, dims, cuts, -0.22, 0.18) * entries
    return jnp.clip(entries, min=-bound, max=bound).astype(kind)


def setup_inputs(seed: int = 0) -> dict:
    streams_of = jax.random.split(jax.random.key(seed), 20)
    return {
        "images": noise(streams_of[0], (IMAGES, SIDE, SIDE, D), 1.0, 6.0, ((0, 32),)),
        "out_grad": noise(streams_of[1], (IMAGES, SIDE, SIDE, D), 1.0, 6.0, ((0, 32),)),
        "image_counts": draw_image_counts(jax.random.fold_in(streams_of[19], 71), 0),
        "regions": draw_regions(jax.random.fold_in(streams_of[19], 71), 0),
        "relative_index": draw_relative_index(jax.random.fold_in(streams_of[19], 71), 0),
        "norm1_gain": jnp.clip(1.0 + 0.1 * jax.random.normal(streams_of[5], (D,), jnp.float32), 0.5, 1.5).astype(jnp.bfloat16),
        "norm1_bias": noise(streams_of[6], (D,), 0.5, 3.0, ((0, 2),)),
        "qkv_weight": noise(streams_of[7], (D, 3 * D), D ** -0.5, 0.25, ((0, 2),)),
        "query_bias": noise(streams_of[8], (D,), 0.5, 3.0, ((0, 2),)),
        "value_bias": noise(streams_of[9], (D,), 0.5, 3.0, ((0, 2),)),
        "bias_table": noise(streams_of[10], (TABLE, HEADS), 1.0, 4.0, ((1, 2),)),
        "proj_weight": noise(streams_of[11], (D, D), (D // 8) ** -0.5, 0.75, ((0, 2),)),
        "proj_bias": noise(streams_of[12], (D,), 0.5, 3.0, ((0, 2),)),
        "norm2_gain": jnp.clip(1.0 + 0.1 * jax.random.normal(streams_of[13], (D,), jnp.float32), 0.5, 1.5).astype(jnp.bfloat16),
        "norm2_bias": noise(streams_of[14], (D,), 0.5, 3.0, ((0, 2),)),
        "fc1_weight": noise(streams_of[15], (D, FF), D ** -0.5, 0.25, ((0, 2),)),
        "fc1_bias": noise(streams_of[16], (FF,), 0.5, 3.0, ((0, 2),)),
        "fc2_weight": noise(streams_of[17], (FF, D), (FF // 2) ** -0.5, 0.1875, ((0, 2),)),
        "fc2_bias": noise(streams_of[18], (D,), 0.5, 3.0, ((0, 2),)),
    }


EPSILON = 1e-05
MASK_FILL = -100.0
HIGH = lax.Precision.HIGHEST

@jax.custom_vjp
def low(v):
    return lax.optimization_barrier(v.astype(jnp.bfloat16)).astype(jnp.float32)

@jax.custom_vjp
def low_back(v):
    return v

def low_keep(v):
    return (low(v), None)

def low_pass(kept, grad):
    return (grad,)

def back_keep(v):
    return (v, None)

def back_low(kept, grad):
    return (low(grad),)
low.defvjp(low_keep, low_pass)
low_back.defvjp(back_keep, back_low)

def to_windows(image):
    count = image.shape[0]
    blocks = SIDE // WIN
    width = image.shape[-1]
    tiles = image.reshape(count, blocks, WIN, blocks, WIN, width).transpose(0, 1, 3, 2, 4, 5)
    return tiles.reshape(count * blocks * blocks, WIN * WIN, width)

def from_windows(tiles, count):
    blocks = SIDE // WIN
    width = tiles.shape[-1]
    image = tiles.reshape(count, blocks, blocks, WIN, WIN, width).transpose(0, 1, 3, 2, 4, 5)
    return image.reshape(count, SIDE, SIDE, width)

def norm_apply(values, gain, offset):
    centred = values - lax.optimization_barrier(jnp.mean(values, axis=-1, keepdims=True))
    spread = lax.optimization_barrier(jnp.mean(centred * centred, axis=-1, keepdims=True))
    return centred * lax.rsqrt(spread + EPSILON) * gain + offset

def window_mask(regions):
    labels = to_windows(regions.reshape(1, SIDE, SIDE, 1))[..., 0]
    differ = labels[:, :, None] != labels[:, None, :]
    return jnp.where(differ, MASK_FILL, 0.0).astype(jnp.float32)

def split_heads(array):
    return array.reshape(array.shape[0], WIN * WIN, HEADS, HEAD)

def block(params, mask_add, relative_index, image):
    norm1_gain, norm1_bias, qkv_weight, query_bias, value_bias, bias_table, proj_weight, proj_bias, norm2_gain, norm2_bias, fc1_weight, fc1_bias, fc2_weight, fc2_bias = params
    count = image.shape[0]
    window_size = WIN * WIN
    normed = low(norm_apply(image, norm1_gain, norm1_bias))
    tiles = to_windows(jnp.roll(normed, (-SHIFT, -SHIFT), axis=(1, 2)))
    mixed = jnp.einsum('tnd,de->tne', tiles, qkv_weight, precision=HIGH)
    query_rows = low_back(low(mixed[..., :D] + query_bias))
    key_rows = low_back(low(mixed[..., D:2 * D]))
    value_rows = low_back(low(mixed[..., 2 * D:] + value_bias))
    position_bias = jnp.transpose(bias_table[relative_index], (2, 0, 1))
    scores = jnp.einsum('tnhe,tmhe->thnm', split_heads(query_rows), split_heads(key_rows), precision=HIGH) * HEAD ** (-0.5)
    scores = scores.reshape(count, -1, HEADS, window_size, window_size) + position_bias + mask_add[:, None]
    scores = low_back(scores.reshape(-1, HEADS, window_size, window_size))
    chance = low(jax.nn.softmax(scores, axis=-1))
    attended = jnp.einsum('thnm,tmhe->tnhe', chance, split_heads(value_rows), precision=HIGH).reshape(-1, window_size, D)
    attended = low_back(low(attended))
    projected = low_back(jnp.einsum('tnd,de->tne', attended, proj_weight, precision=HIGH)) + proj_bias
    branch = jnp.roll(from_windows(projected, count), (SHIFT, SHIFT), axis=(1, 2))
    middle = image + branch
    normed_two = low(norm_apply(middle, norm2_gain, norm2_bias))
    hidden = low_back(jnp.einsum('abcd,df->abcf', normed_two, fc1_weight, precision=HIGH)) + fc1_bias
    activated = low(jax.nn.gelu(hidden, approximate=False))
    return middle + low_back(jnp.einsum('abcf,fd->abcd', activated, fc2_weight, precision=HIGH)) + fc2_bias

def reference(images, out_grad, image_counts, regions, relative_index, norm1_gain, norm1_bias, qkv_weight, query_bias, value_bias, bias_table, proj_weight, proj_bias, norm2_gain, norm2_bias, fc1_weight, fc1_bias, fc2_weight, fc2_bias):
    params = tuple((weight.astype(jnp.float32) for weight in (norm1_gain, norm1_bias, qkv_weight, query_bias, value_bias, bias_table, proj_weight, proj_bias, norm2_gain, norm2_bias, fc1_weight, fc1_bias, fc2_weight, fc2_bias)))
    mask_add = window_mask(regions)
    slots = jnp.arange(IMAGES, dtype=jnp.int32)
    live = (slots % IMG_CAP < image_counts[slots // IMG_CAP]).astype(jnp.float32)
    cotangent = out_grad.astype(jnp.float32) * live[:, None, None, None]

    def layer(inputs, *weights):
        groups = inputs.reshape(-1, 16, SIDE, SIDE, D)
        step = jax.checkpoint(lambda group: block(weights, mask_add, relative_index, group))
        return lax.map(step, groups).reshape(inputs.shape)
    result, pull = jax.vjp(layer, images.astype(jnp.float32), *params)
    grads = pull(cotangent)
    return (result.astype(jnp.bfloat16), grads[0].astype(jnp.bfloat16), grads[1], grads[2], grads[3], grads[4], grads[5], grads[6], grads[7], grads[8], grads[9], grads[10], grads[11], grads[12], grads[13], grads[14])
```

```python
import functools

import jax
import jax.numpy as jnp
import numpy as np
from jax import lax
from jax.experimental import pallas as pl
from jax.experimental.pallas import tpu as pltpu
from jax.sharding import PartitionSpec as P

D = 512
HEADS = 16
HEAD = 32
FF = 2048
SIDE = 14
WIN = 7
SHIFT = 3
TABLE = 169
EPSILON = 1e-05
MASK_FILL = -100.0
PAD_FILL = -1e30
SCALE = HEAD**-0.5
HIGH = lax.Precision.HIGHEST

TOKENS = WIN * WIN
WPAD = 64
WINDOWS = (SIDE // WIN) ** 2
WROWS = WINDOWS * WPAD
SLAB = 16
SROWS = SIDE * SLAB
PACK = 4
GROUPS = HEADS // PACK
GCOLS = PACK * HEAD
LANES = PACK * WPAD
NI = 2
BLOCK = 512
KEEP = 56

f32 = jnp.float32
bf16 = jnp.bfloat16


def window_places():
    take = np.zeros((WROWS, SROWS), np.float32)
    for wr in range(SIDE // WIN):
        for wc in range(SIDE // WIN):
            for i in range(WIN):
                for j in range(WIN):
                    r = (WIN * wr + i + SHIFT) % SIDE
                    c = (WIN * wc + j + SHIFT) % SIDE
                    take[(wr * (SIDE // WIN) + wc) * WPAD + i * WIN + j, r * SLAB + c] = 1
    return take


def dot(a, b):
    return lax.dot_general(a, b, (((1,), (0,)), ((), ())), preferred_element_type=f32)


def dot_nt(a, b):
    return lax.dot_general(a, b, (((1,), (1,)), ((), ())), preferred_element_type=f32)


def dot_tn(a, b):
    return lax.dot_general(a, b, (((0,), (0,)), ((), ())), preferred_element_type=f32)


def normed(x):
    centred = x - jnp.mean(x, axis=-1, keepdims=True)
    rstd = lax.rsqrt(jnp.mean(centred * centred, axis=-1, keepdims=True) + EPSILON)
    return centred * rstd, rstd


def norm_back(grad, gain, hat, rstd):
    g = grad * gain
    mean_g = jnp.mean(g, axis=-1, keepdims=True)
    mean_gh = jnp.mean(g * hat, axis=-1, keepdims=True)
    return rstd * (g - mean_g - hat * mean_gh)


def spread_heads(block, head_mask):
    return jnp.concatenate([block] * PACK, axis=0) * head_mask


def gather_heads(result):
    lane = lax.broadcasted_iota(jnp.int32, (WPAD, GCOLS), 1) // HEAD
    parts = [result[h * WPAD : (h + 1) * WPAD] for h in range(PACK)]
    out = parts[PACK - 1]
    for h in range(PACK - 2, -1, -1):
        out = jnp.where(lane == h, parts[h], out)
    return out


def load_slab(slab, ref):
    slab[:, :, 0:SIDE, :] = ref[...]
    return slab[...].reshape(NI * SROWS, D)


def forward_kernel(
    count_ref, img_ref, og_ref, take_ref, put_ref, qkvw_ref, qb_ref, vb_ref, g1_ref, b1_ref,
    pw_ref, pb_ref, g2_ref, b2_ref, pos_ref, mask_ref, hm_ref,
    qkv_out, prob_out, h1_out, att_out, mid_out, h2_out, cot_out, cotsum_out,
    slab, att,
):
    step = pl.program_id(0)

    @pl.when(step == 0)
    def _():
        slab[...] = jnp.zeros_like(slab)
        cotsum_out[...] = jnp.zeros_like(cotsum_out)

    og = load_slab(slab, og_ref)
    total = jnp.zeros((1, D), f32)
    for i in range(NI):
        live = (step * NI + i < count_ref[0]).astype(f32)
        part = og[i * SROWS : (i + 1) * SROWS].astype(f32) * live
        cot_out[i * SROWS : (i + 1) * SROWS] = part.astype(bf16)
        total = total + jnp.sum(part, axis=0, keepdims=True)
    cotsum_out[...] += total

    x = load_slab(slab, img_ref).astype(f32)
    hat, _ = normed(x)
    h1 = (hat * g1_ref[...] + b1_ref[...]).astype(bf16)
    h1_out[...] = h1
    for i in range(NI):
        tiles = dot(take_ref[...], h1[i * SROWS : (i + 1) * SROWS]).astype(bf16)
        rows = slice(i * WROWS, (i + 1) * WROWS)
        qkv_out[rows, 0:D] = (dot(tiles, qkvw_ref[:, 0:D]) + qb_ref[...]).astype(bf16)
        qkv_out[rows, D : 2 * D] = dot(tiles, qkvw_ref[:, D : 2 * D]).astype(bf16)
        qkv_out[rows, 2 * D : 3 * D] = (
            dot(tiles, qkvw_ref[:, 2 * D : 3 * D]) + vb_ref[...]
        ).astype(bf16)
    head_mask = hm_ref[...]
    for i in range(NI):
        for w in range(WINDOWS):
            rows = slice(i * WROWS + w * WPAD, i * WROWS + (w + 1) * WPAD)
            for g in range(GROUPS):
                cols = slice(g * GCOLS, (g + 1) * GCOLS)
                q = qkv_out[rows, g * GCOLS : (g + 1) * GCOLS]
                k = qkv_out[rows, D + g * GCOLS : D + (g + 1) * GCOLS]
                v = qkv_out[rows, 2 * D + g * GCOLS : 2 * D + (g + 1) * GCOLS]
                s = dot_nt(k, spread_heads(q, head_mask))[:KEEP]
                s = s * SCALE + pos_ref[g] + mask_ref[w]
                e = jnp.exp(s - jnp.max(s, axis=0, keepdims=True))
                p = e / jnp.sum(e, axis=0, keepdims=True)
                p = jnp.concatenate([p, jnp.zeros((WPAD - KEEP, LANES), f32)], axis=0).astype(bf16)
                prob_out[i, w, g] = p
                att[rows, cols] = gather_heads(dot_tn(p, v)).astype(bf16)
    for i in range(NI):
        rows = slice(i * SROWS, (i + 1) * SROWS)
        a = dot(put_ref[...], att[i * WROWS : (i + 1) * WROWS]).astype(bf16)
        att_out[rows] = a
        middle = x[rows] + (dot(a, pw_ref[...]) + pb_ref[...])
        mid_out[rows] = middle
        hat2, _ = normed(middle)
        h2_out[rows] = (hat2 * g2_ref[...] + b2_ref[...]).astype(bf16)


def ffn_kernel(last, *refs):
    if last:
        (h2_ref, cot_ref, f1_ref, fb_ref, f2_ref, mid_ref, f2b_ref, oin_ref, din_ref,
         grads, bias_out, out_ref, dh2_ref, acc1, acc2, oacc, dacc) = refs
    else:
        (h2_ref, cot_ref, f1_ref, fb_ref, f2_ref,
         grads, bias_out, out_ref, dh2_ref, acc1, acc2, oacc, dacc) = refs
    j, c = pl.program_id(0), pl.program_id(1)
    rows = NI * SROWS
    here = pl.ds(pl.multiple_of(c * rows, rows), rows)

    h2 = h2_ref[...]
    cot = cot_ref[...]
    hidden = dot(h2, f1_ref[...]) + fb_ref[0]
    dact = dot_nt(cot, f2_ref[...])
    bell = jnp.exp(hidden * hidden * -0.5)
    base = 1.0 + jnp.abs(hidden) * (0.3275911 * 0.5**0.5)
    t = pl.reciprocal(base, approx=True)
    t = t * (2.0 - base * t)
    half = t * (
        0.127414796
        + t * (-0.142248368 + t * (0.7107068705 + t * (-0.7265760135 + t * 0.5307027145)))
    )
    half = half * bell
    phi = jnp.where(hidden > 0, 1.0 - half, half)
    act = (hidden * phi).astype(bf16)
    dhid = dact * (phi + hidden * bell * 0.3989422804014327)
    dhid_low = dhid.astype(bf16)

    g2 = dot_tn(act, cot)
    g1 = dot_tn(h2, dhid_low)
    fb = jnp.sum(dhid, axis=0, keepdims=True)
    o = dot(act, f2_ref[...])
    d = dot_nt(dhid_low, f1_ref[...])

    @pl.when(c == 0)
    def _():
        acc1[...] = g1
        acc2[...] = g2
        bias_out[0] = fb

    @pl.when(c > 0)
    def _():
        acc1[...] += g1
        acc2[...] += g2
        bias_out[0] += fb

    @pl.when(j == 0)
    def _():
        if last:
            oacc[here] = oin_ref[...] + o
            dacc[here] = din_ref[...] + d
        else:
            oacc[here] = o
            dacc[here] = d

    @pl.when(j == 1)
    def _():
        dh2_ref[...] = dacc[here] + d
        if last:
            res = mid_ref[...] + (oacc[here] + o) + f2b_ref[...]
            out_ref[...] = res.astype(bf16).reshape(NI, SIDE, SLAB, D)[:, :, :SIDE, :]
        else:
            out_ref[...] = oacc[here] + o

    half_rows = D // 2

    @pl.when(c == pl.num_programs(1) - 1)
    def _():
        grads[j, 0:BLOCK] = acc2[...].astype(bf16)
        place = pl.ds(pl.multiple_of(BLOCK + j * half_rows, half_rows), half_rows)
        grads[0, place] = acc1[0:half_rows].astype(bf16)
        grads[1, place] = acc1[half_rows:D].astype(bf16)


def backward_kernel(
    img_ref, cot_ref, dh2_ref, mid_ref, h1_ref, att_ref, qkv_ref, prob_ref,
    take_ref, put_ref, qkvw_ref, pw_ref, g1_ref, g2_ref, hm_ref,
    out_ref, grads, small, bias_out,
    slab, dmix, gq, gp,
):
    step = pl.program_id(0)

    @pl.when(step == 0)
    def _():
        slab[...] = jnp.zeros_like(slab)
        small[...] = jnp.zeros_like(small)
        bias_out[...] = jnp.zeros_like(bias_out)
        gq[...] = jnp.zeros_like(gq)
        gp[...] = jnp.zeros_like(gp)

    hat2, rstd2 = normed(mid_ref[...])
    dh2 = dh2_ref[...]
    small[5:6] += jnp.sum(dh2 * hat2, axis=0, keepdims=True)
    small[6:7] += jnp.sum(dh2, axis=0, keepdims=True)
    dmid = cot_ref[...].astype(f32) + norm_back(dh2, g2_ref[...], hat2, rstd2)
    small[4:5] += jnp.sum(dmid, axis=0, keepdims=True)
    dbr = dmid.astype(bf16)
    gp[...] += dot_tn(att_ref[...], dbr)
    datt = dot_nt(dbr, pw_ref[...]).astype(bf16)
    head_mask = hm_ref[...]
    for i in range(NI):
        dwin = dot(take_ref[...], datt[i * SROWS : (i + 1) * SROWS]).astype(bf16)
        for w in range(WINDOWS):
            rows = slice(i * WROWS + w * WPAD, i * WROWS + (w + 1) * WPAD)
            for g in range(GROUPS):
                cols = slice(g * GCOLS, (g + 1) * GCOLS)
                q = qkv_ref[rows, g * GCOLS : (g + 1) * GCOLS]
                k = qkv_ref[rows, D + g * GCOLS : D + (g + 1) * GCOLS]
                v = qkv_ref[rows, 2 * D + g * GCOLS : 2 * D + (g + 1) * GCOLS]
                p_low = prob_ref[i, w, g]
                p = p_low.astype(f32)[:KEEP]
                da = spread_heads(dwin[w * WPAD : (w + 1) * WPAD, cols], head_mask)
                dp = dot_nt(v, da)[:KEEP]
                dv = dot(p_low, da)
                inner = jnp.sum(dp * p, axis=0, keepdims=True)
                ds = (p * (dp - inner)).astype(bf16).astype(f32)
                bias_out[g] += ds
                ds = jnp.concatenate(
                    [ds, jnp.zeros((WPAD - KEEP, LANES), f32)], axis=0
                ).astype(bf16)
                dk = dot(ds, spread_heads(q, head_mask)) * SCALE
                dq = gather_heads(dot_tn(ds, k)) * SCALE
                dmix[rows, g * GCOLS : (g + 1) * GCOLS] = dq.astype(bf16)
                dmix[rows, D + g * GCOLS : D + (g + 1) * GCOLS] = dk.astype(bf16)
                dmix[rows, 2 * D + g * GCOLS : 2 * D + (g + 1) * GCOLS] = dv.astype(bf16)
    small[2:3] += jnp.sum(dmix[:, 0:D].astype(f32), axis=0, keepdims=True)
    small[3:4] += jnp.sum(dmix[:, 2 * D : 3 * D].astype(f32), axis=0, keepdims=True)

    x = load_slab(slab, img_ref).astype(f32)
    hat1, rstd1 = normed(x)
    for i in range(NI):
        rows = slice(i * SROWS, (i + 1) * SROWS)
        dm = dot(put_ref[...], dmix[i * WROWS : (i + 1) * WROWS]).astype(bf16)
        gq[...] += dot_tn(h1_ref[rows], dm)
        dh1 = dot_nt(dm, qkvw_ref[...])
        small[0:1] += jnp.sum(dh1 * hat1[rows], axis=0, keepdims=True)
        small[1:2] += jnp.sum(dh1, axis=0, keepdims=True)
        gx = dmid[rows] + norm_back(dh1, g1_ref[...], hat1[rows], rstd1[rows])
        out_ref[i] = gx.astype(bf16).reshape(SIDE, SLAB, D)[:, :SIDE, :]

    @pl.when(step == pl.num_programs(0) - 1)
    def _():
        half = D // 2
        for o in range(2):
            rows = slice(o * half, (o + 1) * half)
            for b in range(3):
                grads[o, b * half : (b + 1) * half] = gq[rows, b * D : (b + 1) * D].astype(bf16)
            grads[o, 3 * half : 4 * half] = gp[rows].astype(bf16)


def whole(shape):
    return pl.BlockSpec(shape, lambda *_: (0,) * len(shape))


def params(axes, flops, size):
    return dict(
        compiler_params=pltpu.CompilerParams(
            dimension_semantics=("arbitrary",) * axes, vmem_limit_bytes=60 * 1024 * 1024
        ),
        cost_estimate=pl.CostEstimate(flops=int(flops), bytes_accessed=int(size), transcendentals=0),
    )


def run_forward(images, out_grad, count, take, put, qkvw, qb, vb, g1, b1, pw, pb, g2, b2, pos, mask, hm):
    n = images.shape[0]
    img = pl.BlockSpec((NI, SIDE, SIDE, D), lambda i: (i, 0, 0, 0))
    srow = pl.BlockSpec((NI * SROWS, D), lambda i: (i, 0))
    row = whole((1, D))
    slab_shape = jax.ShapeDtypeStruct((n * SROWS, D), bf16)
    return pl.pallas_call(
        forward_kernel,
        grid=(n // NI,),
        in_specs=[
            pl.BlockSpec(memory_space=pltpu.SMEM), img, img, whole(take.shape), whole(put.shape),
            whole(qkvw.shape), row, row, row, row, whole(pw.shape), row, row, row,
            whole(pos.shape), whole(mask.shape), whole(hm.shape),
        ],
        out_specs=[
            pl.BlockSpec((NI * WROWS, 3 * D), lambda i: (i, 0)),
            pl.BlockSpec((NI, WINDOWS, GROUPS, WPAD, LANES), lambda i: (i, 0, 0, 0, 0)),
            srow, srow, srow, srow, srow, row,
        ],
        out_shape=[
            jax.ShapeDtypeStruct((n * WROWS, 3 * D), bf16),
            jax.ShapeDtypeStruct((n, WINDOWS, GROUPS, WPAD, LANES), bf16),
            slab_shape, slab_shape, jax.ShapeDtypeStruct((n * SROWS, D), f32), slab_shape, slab_shape,
            jax.ShapeDtypeStruct((1, D), f32),
        ],
        scratch_shapes=[
            pltpu.VMEM((NI, SIDE, SLAB, D), bf16),
            pltpu.VMEM((NI * WROWS, D), bf16),
        ],
        name="forward_attention",
        **params(1, n * 1.0e9, n * 3e6),
    )(count, images, out_grad, take, put, qkvw, qb, vb, g1, b1, pw, pb, g2, b2, pos, mask, hm)


def run_ffn(which, h2, cot, fc1, fb, fc2, extra):
    rows = NI * SROWS
    steps = h2.shape[0] // rows
    last = extra is not None
    chunk = pl.BlockSpec((rows, D), lambda j, c: (c, 0))
    late = pl.BlockSpec((rows, D), lambda j, c: (c * j, 0))
    early = pl.BlockSpec((rows, D), lambda j, c: (c * (1 - j) + (steps - 1) * j, 0))
    in_specs = [
        chunk, chunk,
        pl.BlockSpec((D, BLOCK), lambda j, c: (0, 2 * j + which)),
        pl.BlockSpec((1, 1, BLOCK), lambda j, c: (2 * j + which, 0, 0)),
        pl.BlockSpec((BLOCK, D), lambda j, c: (2 * j + which, 0)),
    ]
    args = [h2, cot, fc1, fb.reshape(-1, 1, BLOCK), fc2]
    acc = jax.ShapeDtypeStruct(h2.shape, f32)
    if last:
        in_specs += [late, whole((1, D)), early, early]
        args += list(extra)
        out = jax.ShapeDtypeStruct((steps * NI, SIDE, SIDE, D), bf16)
        out_spec = pl.BlockSpec((NI, SIDE, SIDE, D), lambda j, c: (c * j, 0, 0, 0))
    else:
        out, out_spec = acc, late
    return pl.pallas_call(
        functools.partial(ffn_kernel, last),
        grid=(2, steps),
        in_specs=in_specs,
        out_specs=[
            whole((2, 2 * BLOCK, D)), pl.BlockSpec((1, 1, BLOCK), lambda j, c: (j, 0, 0)), out_spec, late,
        ],
        out_shape=[
            jax.ShapeDtypeStruct((2, 2 * BLOCK, D), bf16),
            jax.ShapeDtypeStruct((2, 1, BLOCK), f32), out, acc,
        ],
        scratch_shapes=[
            pltpu.VMEM((D, BLOCK), f32), pltpu.VMEM((BLOCK, D), f32),
            pltpu.VMEM(h2.shape, f32), pltpu.VMEM(h2.shape, f32),
        ],
        name="ffn",
        **params(2, 2 * 12 * h2.shape[0] * D * BLOCK, 20e6),
    )(*args)


def run_backward(images, cot, dh2, mid, h1, att, qkv, prob, take, put, qkvw, pw, g1, g2, hm):
    n = images.shape[0]
    img = pl.BlockSpec((NI, SIDE, SIDE, D), lambda i: (i, 0, 0, 0))
    srow = pl.BlockSpec((NI * SROWS, D), lambda i: (i, 0))
    row = whole((1, D))
    return pl.pallas_call(
        backward_kernel,
        grid=(n // NI,),
        in_specs=[
            img, srow, srow, srow, srow, srow,
            pl.BlockSpec((NI * WROWS, 3 * D), lambda i: (i, 0)),
            pl.BlockSpec((NI, WINDOWS, GROUPS, WPAD, LANES), lambda i: (i, 0, 0, 0, 0)),
            whole(take.shape), whole(put.shape), whole(qkvw.shape), whole(pw.shape), row, row,
            whole(hm.shape),
        ],
        out_specs=[img, whole((2, 2 * D, D)), whole((8, D)), whole((GROUPS, KEEP, LANES))],
        out_shape=[
            jax.ShapeDtypeStruct(images.shape, bf16),
            jax.ShapeDtypeStruct((2, 2 * D, D), bf16),
            jax.ShapeDtypeStruct((8, D), f32),
            jax.ShapeDtypeStruct((GROUPS, KEEP, LANES), f32),
        ],
        scratch_shapes=[
            pltpu.VMEM((NI, SIDE, SLAB, D), bf16),
            pltpu.VMEM((NI * WROWS, 3 * D), bf16),
            pltpu.VMEM((D, 3 * D), f32),
            pltpu.VMEM((D, D), f32),
        ],
        name="backward_attention",
        **params(1, n * 2.5e9, n * 3e6),
    )(images, cot, dh2, mid, h1, att, qkv, prob, take, put, qkvw, pw, g1, g2, hm)


def digits_of(n):
    digits, stride = [], 1
    while n > 1:
        base = 4 if n % 4 == 0 else 2
        digits.append((base, stride))
        stride *= base
        n //= base
    return digits


def make_shards(replicas):
    axes = ("replica", "shard")
    core_pairs = [(r * 2 + s, r * 2 + 1 - s) for r in range(replicas) for s in range(2)]
    digits = digits_of(replicas)

    def across(value):
        return lax.ppermute(value, axes, core_pairs)

    def partner(value, k, stride):
        pairs = [(r * 2 + s, (r ^ (k * stride)) * 2 + s) for r in range(replicas) for s in range(2)]
        return lax.ppermute(value, axes, pairs)

    def place(base, stride):
        return (lax.axis_index("replica") // stride) % base

    def pick(value, index):
        return lax.dynamic_index_in_dim(value, index, 0, keepdims=False)

    def in_order(parts, mine):
        base = len(parts)
        laid = []
        for at in range(base):
            value = parts[at]
            for c in range(1, base):
                value = jnp.where(mine == c, parts[at ^ c], value)
            laid.append(value)
        return jnp.stack(laid)

    def both_halves(value):
        other = across(value)
        first = lax.axis_index("shard") == 0
        return jnp.where(first, value, other), jnp.where(first, other, value)

    def reduce_grads(grads):
        s = lax.axis_index("shard")
        got = across(pick(grads, 1 - s))
        buf = (pick(grads, s).astype(f32) + got.astype(f32)).astype(bf16)
        for base, stride in digits:
            mine = place(base, stride)
            view = buf.reshape(base, buf.shape[0] // base, buf.shape[1])
            total = pick(view, mine).astype(f32)
            for k in range(1, base):
                total = total + partner(pick(view, mine ^ k), k, stride).astype(f32)
            buf = total.astype(bf16)
        for base, stride in reversed(digits):
            parts = [buf] + [partner(buf, k, stride) for k in range(1, base)]
            buf = in_order(parts, place(base, stride)).reshape(-1, buf.shape[1])
        return buf.astype(f32)

    def reduce_small(value):
        value = value + across(value)
        for base, stride in digits:
            total = value
            for k in range(1, base):
                total = total + partner(value, k, stride)
            value = total
        return value

    def shards(
        images, out_grad, image_counts, regions, relative_index,
        norm1_gain, norm1_bias, qkv_weight, query_bias, value_bias, bias_table,
        proj_weight, proj_bias, norm2_gain, norm2_bias, fc1_weight, fc1_bias, fc2_weight, fc2_bias,
    ):
        shard = lax.axis_index("shard")
        half = D // 2
        qkvw = jnp.concatenate(both_halves(qkv_weight), axis=0)
        vectors = [
            norm1_gain, norm1_bias, query_bias, value_bias,
            proj_bias, norm2_gain, norm2_bias, fc2_bias,
        ]
        table_flat = jnp.pad(bias_table.T, ((0, 0), (0, half - TABLE)))
        packed = jnp.concatenate(
            [jnp.stack(vectors), fc1_bias.reshape(-1, half), table_flat], axis=0
        )
        low_part, high_part = both_halves(packed)
        joined = jnp.concatenate([low_part[:8], high_part[:8]], axis=1).astype(f32)
        g1, b1, qb, vb, pb, g2, b2, f2b = [joined[i : i + 1] for i in range(8)]
        fb = jnp.concatenate(
            [low_part[8:12].reshape(1, -1), high_part[8:12].reshape(1, -1)], axis=1
        ).astype(f32)
        table = jnp.concatenate([low_part[12:, :TABLE], high_part[12:, :TABLE]], axis=0)
        pw = jnp.concatenate(both_halves(proj_weight), axis=0)
        fc1 = jnp.concatenate(both_halves(fc1_weight), axis=0)
        fc2 = jnp.concatenate(both_halves(fc2_weight), axis=0)

        index = jnp.pad(
            relative_index.T, ((0, KEEP - TOKENS), (0, WPAD - TOKENS)), constant_values=-1
        )
        onehot = (
            index.reshape(1, -1) == jnp.arange(TABLE, dtype=jnp.int32)[:, None]
        ).astype(bf16)
        pos = dot(table, onehot).reshape(GROUPS, PACK, KEEP, WPAD)
        pos = pos.transpose(0, 2, 1, 3).reshape(GROUPS, KEEP, LANES)
        labels = regions.reshape(SIDE // WIN, WIN, SIDE // WIN, WIN).transpose(0, 2, 1, 3)
        labels = labels.reshape(WINDOWS, TOKENS)
        differ = labels[:, :, None] != labels[:, None, :]
        mask = jnp.where(differ, MASK_FILL, 0.0).astype(f32)
        mask = jnp.pad(mask, ((0, 0), (0, 0), (0, WPAD - TOKENS)))
        mask = jnp.pad(mask, ((0, 0), (0, KEEP - TOKENS), (0, 0)), constant_values=PAD_FILL)
        mask = jnp.tile(mask, (1, 1, PACK))

        take_np = window_places()
        take = jnp.asarray(take_np, bf16)
        put = jnp.asarray(take_np.T, bf16)
        hm = jnp.asarray(
            (np.arange(LANES)[:, None] // WPAD) == (np.arange(GCOLS)[None, :] // HEAD), bf16
        )

        qkv, prob, h1, att, mid, h2, cot, cotsum = run_forward(
            images, out_grad, image_counts, take, put, qkvw, qb, vb, g1, b1,
            pw, pb, g2, b2, pos, mask, hm,
        )
        grads_a, fbias_a, oacc, dacc = run_ffn(0, h2, cot, fc1, fb, fc2, None)
        grads_b, fbias_b, output, dh2 = run_ffn(1, h2, cot, fc1, fb, fc2, (mid, f2b, oacc, dacc))
        grad_images, grads_c, small, bias_sum = run_backward(
            images, cot, dh2, mid, h1, att, qkv, prob, take, put, qkvw, pw, g1, g2, hm
        )
        sum_a = reduce_grads(grads_a)
        sum_b = reduce_grads(grads_b)

        by_head = bias_sum.reshape(GROUPS, KEEP, PACK, WPAD).transpose(0, 2, 1, 3)
        table_grad = lax.dot_general(
            by_head.reshape(HEADS, -1), onehot.astype(f32), (((1,), (1,)), ((), ())),
            precision=HIGH, preferred_element_type=f32,
        )
        table_rows = jnp.pad(table_grad, ((0, 0), (0, half - TABLE))).reshape(-1, D)
        fbias = jnp.concatenate([fbias_a, fbias_b], axis=1).reshape(2 * 2, BLOCK)
        vector = jnp.concatenate([small[0:7], cotsum, fbias, table_rows], axis=0)
        vector = reduce_small(vector)
        sum_c = reduce_grads(grads_c)

        own = lax.dynamic_slice(vector, (0, shard * half), (8, half))
        own_fb = lax.dynamic_slice(vector, (8 + 2 * shard, 0), (2, BLOCK)).reshape(-1)
        rows = HEADS * half // D
        own_table = lax.dynamic_slice(
            vector, (12 + shard * (rows // 2), 0), (rows // 2, D)
        ).reshape(HEADS // 2, half)[:, :TABLE].T
        grad_fc2 = jnp.concatenate([sum_a[:BLOCK], sum_b[:BLOCK]], axis=0)
        grad_fc1 = jnp.concatenate(
            [sum_a[BLOCK : BLOCK + half], sum_b[BLOCK : BLOCK + half],
             sum_a[BLOCK + half :], sum_b[BLOCK + half :]], axis=1,
        )
        grad_qkv = jnp.concatenate([sum_c[b * half : (b + 1) * half] for b in range(3)], axis=1)
        return (
            output, grad_images, own[0], own[1], grad_qkv, own[2], own[3], own_table,
            sum_c[3 * half :], own[4], own[5], own[6], grad_fc1, own_fb, grad_fc2, own[7],
        )

    return shards


def solution(mesh):
    return jax.shard_map(
        make_shards(mesh.shape["replica"]),
        mesh=mesh,
        in_specs=(
            P(("replica", "shard"), None, None, None),
            P(("replica", "shard"), None, None, None),
            P(("replica", "shard")),
            P(),
            P(),
            P("shard"),
            P("shard"),
            P("shard", None),
            P("shard"),
            P("shard"),
            P(None, "shard"),
            P("shard", None),
            P("shard"),
            P("shard"),
            P("shard"),
            P("shard", None),
            P("shard"),
            P("shard", None),
            P("shard"),
        ),
        out_specs=(
            P(("replica", "shard"), None, None, None),
            P(("replica", "shard"), None, None, None),
            P("shard"),
            P("shard"),
            P("shard", None),
            P("shard"),
            P("shard"),
            P(None, "shard"),
            P("shard", None),
            P("shard"),
            P("shard"),
            P("shard"),
            P("shard", None),
            P("shard"),
            P("shard", None),
            P("shard"),
        ),
        check_vma=False,
    )
```

```python
import functools

import jax
import jax.numpy as jnp
import numpy as np
from jax import lax
from jax.experimental import pallas as pl
from jax.experimental.pallas import tpu as pltpu
from jax.sharding import PartitionSpec as P

D = 512
HEADS = 16
HEAD = 32
FF = 2048
SIDE = 14
WIN = 7
SHIFT = 3
TABLE = 169
EPSILON = 1e-05
MASK_FILL = -100.0
PAD_FILL = -1e30
SCALE = HEAD**-0.5
HIGH = lax.Precision.HIGHEST

TOKENS = WIN * WIN
CELLS = SIDE // WIN
WINDOWS = CELLS**2
IMGS = 8
WPAD = 64
WROWS = IMGS * WPAD
DROWS = TOKENS * IMGS
PACK = 4
GROUPS = HEADS // PACK
GCOLS = PACK * HEAD
LANES = PACK * WPAD
SPLIT = 2
PART = GROUPS // SPLIT
PCOLS = PART * GCOLS
BLOCK = 512
KEEP = 56

f32 = jnp.float32
bf16 = jnp.bfloat16


def window_places():
    take = np.zeros((WROWS, DROWS), np.float32)
    for i in range(IMGS):
        for t in range(TOKENS):
            take[i * WPAD + t, t * IMGS + i] = 1
    return take


def dot(a, b):
    return lax.dot_general(a, b, (((1,), (0,)), ((), ())), preferred_element_type=f32)


def dot_nt(a, b):
    return lax.dot_general(a, b, (((1,), (1,)), ((), ())), preferred_element_type=f32)


def dot_tn(a, b):
    return lax.dot_general(a, b, (((0,), (0,)), ((), ())), preferred_element_type=f32)


def normed(x):
    centred = x - jnp.mean(x, axis=-1, keepdims=True)
    rstd = lax.rsqrt(jnp.mean(centred * centred, axis=-1, keepdims=True) + EPSILON)
    return centred * rstd, rstd


def norm_back(grad, gain, hat, rstd):
    g = grad * gain
    mean_g = jnp.mean(g, axis=-1, keepdims=True)
    mean_gh = jnp.mean(g * hat, axis=-1, keepdims=True)
    return rstd * (g - mean_g - hat * mean_gh)


def spread_heads(block, head_mask):
    return jnp.concatenate([block] * PACK, axis=0) * head_mask


def gather_heads(result):
    lane = lax.broadcasted_iota(jnp.int32, (WPAD, GCOLS), 1) // HEAD
    parts = [result[h * WPAD : (h + 1) * WPAD] for h in range(PACK)]
    out = parts[PACK - 1]
    for h in range(PACK - 2, -1, -1):
        out = jnp.where(lane == h, parts[h], out)
    return out


def token_places(place):
    row0 = (place // CELLS) * WIN + SHIFT
    col0 = (place % CELLS) * WIN + SHIFT
    for i in range(WIN):
        r = row0 + i
        r = jnp.where(r >= SIDE, r - SIDE, r)
        for j in range(WIN):
            c = col0 + j
            yield (i * WIN + j) * IMGS, r, jnp.where(c >= SIDE, c - SIDE, c)


def load_window(rows, ref, place):
    for at, r, c in token_places(place):
        rows[at : at + IMGS] = ref[r, c].astype(f32)
    return rows[...]


def store_window(ref, value, place):
    for at, r, c in token_places(place):
        ref[r, c] = value[at : at + IMGS].astype(bf16)


def join_rows(full, own_ref, other_ref):
    half = full.shape[0] // 2
    first = lax.axis_index("shard") == 0

    @pl.when(first)
    def _():
        full[0:half] = own_ref[...]
        full[half:] = other_ref[...]

    @pl.when(jnp.logical_not(first))
    def _():
        full[0:half] = other_ref[...]
        full[half:] = own_ref[...]


def join_vectors(vec, own_ref, other_ref):
    first = lax.axis_index("shard") == 0
    own, other = own_ref[...].astype(f32), other_ref[...].astype(f32)
    vec[:, 0 : D // 2] = jnp.where(first, own, other)
    vec[:, D // 2 :] = jnp.where(first, other, own)


G1, B1, QB, VB, PB, G2, B2, F2B, FB = range(9)
VROWS = 12


def forward_kernel(
    count_ref, img_ref, og_ref, take_ref, put_ref, qw0_ref, qw1_ref, pw0_ref, pw1_ref,
    vec0_ref, vec1_ref, pos_ref, mask_ref, hm_ref,
    qkv_out, prob_out, h1_out, att_out, mid_out, h2_out, cot_out, cotsum_out,
    rows_in, att, qkvw_ref, pw_ref, vec,
):
    place = pl.program_id(0)

    @pl.when(place == 0)
    def _():
        cotsum_out[...] = jnp.zeros_like(cotsum_out)
        join_rows(qkvw_ref, qw0_ref, qw1_ref)
        join_rows(pw_ref, pw0_ref, pw1_ref)
        join_vectors(vec, vec0_ref, vec1_ref)

    def row(at):
        return vec[at : at + 1]

    image = lax.broadcasted_iota(jnp.int32, (DROWS, D), 0) % IMGS
    cot = jnp.where(image < count_ref[0], load_window(rows_in, og_ref, place), 0.0)
    cot_out[...] = cot.astype(bf16)
    cotsum_out[...] += jnp.sum(cot, axis=0, keepdims=True)

    x = load_window(rows_in, img_ref, place)
    hat, _ = normed(x)
    h1 = (hat * row(G1) + row(B1)).astype(bf16)
    h1_out[...] = h1
    tiles = dot(take_ref[...], h1).astype(bf16)
    qkv_out[:, 0:D] = (dot(tiles, qkvw_ref[:, 0:D]) + row(QB)).astype(bf16)
    qkv_out[:, D : 2 * D] = dot(tiles, qkvw_ref[:, D : 2 * D]).astype(bf16)
    qkv_out[:, 2 * D : 3 * D] = (dot(tiles, qkvw_ref[:, 2 * D : 3 * D]) + row(VB)).astype(bf16)
    head_mask = hm_ref[...]
    for i in range(IMGS):
        rows = slice(i * WPAD, (i + 1) * WPAD)
        for g in range(GROUPS):
            cols = slice(g * GCOLS, (g + 1) * GCOLS)
            q = qkv_out[rows, g * GCOLS : (g + 1) * GCOLS]
            k = qkv_out[rows, D + g * GCOLS : D + (g + 1) * GCOLS]
            v = qkv_out[rows, 2 * D + g * GCOLS : 2 * D + (g + 1) * GCOLS]
            s = dot_nt(k, spread_heads(q, head_mask))[:KEEP]
            s = s * SCALE + pos_ref[g] + mask_ref[...]
            e = jnp.exp(s - jnp.max(s, axis=0, keepdims=True))
            p = e / jnp.sum(e, axis=0, keepdims=True)
            p = jnp.concatenate([p, jnp.zeros((WPAD - KEEP, LANES), f32)], axis=0).astype(bf16)
            prob_out[g, i] = p
            att[rows, cols] = gather_heads(dot_tn(p, v)).astype(bf16)
    a = dot(put_ref[...], att[...]).astype(bf16)
    att_out[...] = a
    middle = x + (dot(a, pw_ref[...]) + row(PB))
    mid_out[...] = middle
    hat2, _ = normed(middle)
    h2_out[...] = (hat2 * row(G2) + row(B2)).astype(bf16)


def ffn_kernel(which, last, *refs):
    refs = list(refs)
    h2_ref, cot_ref, f10_ref, f11_ref, f20_ref, f21_ref, vec0_ref, vec1_ref = refs[:8]
    refs = refs[8:]
    if last:
        oin_ref, din_ref, mid_ref = refs[:3]
        refs = refs[3:]
    grads, bias_out, out_ref, dh2_ref, acc1, acc2, oacc, dacc, f1_ref, f2_ref, vec, fbias = refs
    j, c = pl.program_id(0), pl.program_id(1)

    @pl.when(c == 0)
    def _():
        mine = lax.axis_index("shard") == j
        join_rows(f1_ref, f10_ref, f11_ref)
        join_vectors(vec, vec0_ref, vec1_ref)

        def owner_parts(f2, vectors):
            f2_ref[...] = f2[...]
            for b in range(BLOCK // (D // 2)):
                at = FB + which * (BLOCK // (D // 2)) + b
                fbias[:, b * D // 2 : (b + 1) * D // 2] = vectors[at : at + 1].astype(f32)

        @pl.when(mine)
        def _():
            owner_parts(f20_ref, vec0_ref)

        @pl.when(jnp.logical_not(mine))
        def _():
            owner_parts(f21_ref, vec1_ref)

    h2 = h2_ref[...]
    cot = cot_ref[...]
    hidden = dot(h2, f1_ref[...]) + fbias[...]
    dact = dot_nt(cot, f2_ref[...])
    bell = jnp.exp(hidden * hidden * -0.5)
    base = 1.0 + jnp.abs(hidden) * (0.3275911 * 0.5**0.5)
    t = pl.reciprocal(base, approx=True)
    t = t * (2.0 - base * t)
    half = t * (
        0.127414796
        + t * (-0.142248368 + t * (0.7107068705 + t * (-0.7265760135 + t * 0.5307027145)))
    )
    half = half * bell
    phi = jnp.where(hidden > 0, 1.0 - half, half)
    act = (hidden * phi).astype(bf16)
    dhid = dact * (phi + hidden * bell * 0.3989422804014327)
    dhid_low = dhid.astype(bf16)

    g2 = dot_tn(act, cot)
    g1 = dot_tn(h2, dhid_low)
    fb = jnp.sum(dhid, axis=0, keepdims=True)
    o = dot(act, f2_ref[...])
    d = dot_nt(dhid_low, f1_ref[...])

    @pl.when(c == 0)
    def _():
        acc1[...] = g1
        acc2[...] = g2
        bias_out[0] = fb

    @pl.when(c > 0)
    def _():
        acc1[...] += g1
        acc2[...] += g2
        bias_out[0] += fb

    @pl.when(j == 0)
    def _():
        oacc[c] = o
        dacc[c] = d

    @pl.when(j == 1)
    def _():
        if last:
            dh2_ref[...] = dacc[c] + d + din_ref[...]
            full = mid_ref[...] + (oacc[c] + o + oin_ref[...]) + vec[F2B : F2B + 1]
            store_window(out_ref, full, c)
        else:
            dh2_ref[...] = dacc[c] + d
            out_ref[...] = oacc[c] + o

    half_rows = D // 2

    @pl.when(c == pl.num_programs(1) - 1)
    def _():
        grads[j, 0:BLOCK] = acc2[...].astype(bf16)
        place = pl.ds(pl.multiple_of(BLOCK + j * half_rows, half_rows), half_rows)
        grads[0, place] = acc1[0:half_rows].astype(bf16)
        grads[1, place] = acc1[half_rows:D].astype(bf16)


def middle_kernel(
    cot_ref, dh2_ref, mid_ref, att_ref, take_ref, pw0_ref, pw1_ref, vec0_ref, vec1_ref,
    dmid_out, dwin_out, grads, small, gp, pw_ref, vec,
):
    place = pl.program_id(0)

    @pl.when(place == 0)
    def _():
        small[...] = jnp.zeros_like(small)
        gp[...] = jnp.zeros_like(gp)
        join_rows(pw_ref, pw0_ref, pw1_ref)
        join_vectors(vec, vec0_ref, vec1_ref)

    hat2, rstd2 = normed(mid_ref[...])
    dh2 = dh2_ref[...]
    small[0:1] += jnp.sum(dh2 * hat2, axis=0, keepdims=True)
    small[1:2] += jnp.sum(dh2, axis=0, keepdims=True)
    dmid = cot_ref[...].astype(f32) + norm_back(dh2, vec[G2 : G2 + 1], hat2, rstd2)
    small[2:3] += jnp.sum(dmid, axis=0, keepdims=True)
    dmid_out[...] = dmid
    dbr = dmid.astype(bf16)
    gp[...] += dot_tn(att_ref[...], dbr)
    datt = dot_nt(dbr, pw_ref[...]).astype(bf16)
    dwin_out[...] = dot(take_ref[...], datt).astype(bf16)

    @pl.when(place == pl.num_programs(0) - 1)
    def _():
        half = D // 2
        for o in range(2):
            for b in range(2):
                grads[o, b * half : (b + 1) * half] = gp[
                    o * half : (o + 1) * half, b * half : (b + 1) * half
                ].astype(bf16)


def heads_kernel(
    q_ref, k_ref, v_ref, prob_ref, dwin_ref, h1_ref, put_ref, hm_ref,
    dm_out, grads, small, bias_out, dmix, gq,
):
    place = pl.program_id(0)

    @pl.when(place == 0)
    def _():
        small[...] = jnp.zeros_like(small)
        bias_out[...] = jnp.zeros_like(bias_out)
        gq[...] = jnp.zeros_like(gq)

    head_mask = hm_ref[...]
    for g in range(PART):
        cols = slice(g * GCOLS, (g + 1) * GCOLS)
        for i in range(IMGS):
            rows = slice(i * WPAD, (i + 1) * WPAD)
            q = q_ref[rows, cols]
            k = k_ref[rows, cols]
            v = v_ref[rows, cols]
            p_low = prob_ref[g, i]
            p = p_low.astype(f32)[:KEEP]
            da = spread_heads(dwin_ref[rows, cols], head_mask)
            dp = dot_nt(v, da)[:KEEP]
            dv = dot(p_low, da)
            inner = jnp.sum(dp * p, axis=0, keepdims=True)
            ds = (p * (dp - inner)).astype(bf16).astype(f32)
            bias_out[g] += ds
            ds = jnp.concatenate([ds, jnp.zeros((WPAD - KEEP, LANES), f32)], axis=0).astype(bf16)
            dk = dot(ds, spread_heads(q, head_mask)) * SCALE
            dq = gather_heads(dot_tn(ds, k)) * SCALE
            dmix[rows, g * GCOLS : (g + 1) * GCOLS] = dq.astype(bf16)
            dmix[rows, PCOLS + g * GCOLS : PCOLS + (g + 1) * GCOLS] = dk.astype(bf16)
            dmix[rows, 2 * PCOLS + g * GCOLS : 2 * PCOLS + (g + 1) * GCOLS] = dv.astype(bf16)
    small[0:1] += jnp.sum(dmix[:, 0:PCOLS].astype(f32), axis=0, keepdims=True)
    small[1:2] += jnp.sum(dmix[:, 2 * PCOLS : 3 * PCOLS].astype(f32), axis=0, keepdims=True)
    dm = dot(put_ref[...], dmix[...]).astype(bf16)
    dm_out[...] = dm
    gq[...] += dot_tn(h1_ref[...], dm)

    @pl.when(place == pl.num_programs(0) - 1)
    def _():
        half = D // 2
        for o in range(2):
            for b in range(3):
                grads[o, b * half : (b + 1) * half] = gq[
                    o * half : (o + 1) * half, b * PCOLS : (b + 1) * PCOLS
                ].astype(bf16)


def final_kernel(
    img_ref, dmid_ref, dm0_ref, dm1_ref, qw0_ref, qw1_ref, vec0_ref, vec1_ref,
    out_ref, small, rows_in, qkvw_ref, vec,
):
    place = pl.program_id(0)

    @pl.when(place == 0)
    def _():
        small[...] = jnp.zeros_like(small)
        join_rows(qkvw_ref, qw0_ref, qw1_ref)
        join_vectors(vec, vec0_ref, vec1_ref)

    dh1 = None
    for part, ref in enumerate((dm0_ref, dm1_ref)):
        for b in range(3):
            at = b * D + part * PCOLS
            term = dot_nt(ref[:, b * PCOLS : (b + 1) * PCOLS], qkvw_ref[:, at : at + PCOLS])
            dh1 = term if dh1 is None else dh1 + term
    hat1, rstd1 = normed(load_window(rows_in, img_ref, place))
    small[0:1] += jnp.sum(dh1 * hat1, axis=0, keepdims=True)
    small[1:2] += jnp.sum(dh1, axis=0, keepdims=True)
    store_window(out_ref, dmid_ref[...] + norm_back(dh1, vec[G1 : G1 + 1], hat1, rstd1), place)


def whole(shape):
    return pl.BlockSpec(shape, lambda *_: (0,) * len(shape))


def by_place(*dims):
    return pl.BlockSpec((None,) + dims, lambda i: (i,) + (0,) * len(dims))


def params(axes, flops, size):
    return dict(
        compiler_params=pltpu.CompilerParams(
            dimension_semantics=("arbitrary",) * axes, vmem_limit_bytes=60 * 1024 * 1024
        ),
        cost_estimate=pl.CostEstimate(flops=int(flops), bytes_accessed=int(size), transcendentals=0),
    )


IMAGE = (SIDE, SIDE, IMGS, D)


def dense(kind, cols=D):
    return jax.ShapeDtypeStruct((WINDOWS, DROWS, cols), kind)


VECTORS = pltpu.VMEM((VROWS, D), f32)


def run_forward(images, out_grad, count, take, put, qkvw, pw, vec, pos, mask, hm):
    drow = by_place(DROWS, D)
    pair = [whole(qkvw[0].shape)] * 2 + [whole(pw[0].shape)] * 2 + [whole(vec[0].shape)] * 2
    return pl.pallas_call(
        forward_kernel,
        grid=(WINDOWS,),
        in_specs=[
            pl.BlockSpec(memory_space=pltpu.SMEM), whole(IMAGE), whole(IMAGE),
            whole(take.shape), whole(put.shape), *pair,
            whole(pos.shape), by_place(KEEP, LANES), whole(hm.shape),
        ],
        out_specs=[
            by_place(WROWS, 3 * D), by_place(GROUPS, IMGS, WPAD, LANES),
            drow, drow, drow, drow, drow, whole((1, D)),
        ],
        out_shape=[
            jax.ShapeDtypeStruct((WINDOWS, WROWS, 3 * D), bf16),
            jax.ShapeDtypeStruct((WINDOWS, GROUPS, IMGS, WPAD, LANES), bf16),
            dense(bf16), dense(bf16), dense(f32), dense(bf16), dense(bf16),
            jax.ShapeDtypeStruct((1, D), f32),
        ],
        scratch_shapes=[
            pltpu.VMEM((DROWS, D), f32), pltpu.VMEM((WROWS, D), bf16),
            pltpu.VMEM((D, 3 * D), bf16), pltpu.VMEM((D, D), bf16), VECTORS,
        ],
        name="forward_attention",
        **params(1, 9e9, 25e6),
    )(count, images, out_grad, take, put, *qkvw, *pw, *vec, pos, mask, hm)


def run_ffn(which, h2, cot, fc1, fc2, vec, finish=None):
    last = finish is not None
    chunk = pl.BlockSpec((None, DROWS, D), lambda j, c: (c, 0, 0))
    late = pl.BlockSpec((None, DROWS, D), lambda j, c: (c * j, 0, 0))
    f1 = pl.BlockSpec((D // 2, BLOCK), lambda j, c: (0, 2 * j + which))
    f2 = pl.BlockSpec((BLOCK, D), lambda j, c: (which, 0))
    vecs = whole(vec[0].shape)
    in_specs = [chunk, chunk, f1, f1, f2, f2, vecs, vecs]
    args = [h2, cot, *fc1, *fc2, *vec]
    out, out_spec = dense(f32), late
    if last:
        in_specs += [late, late, late]
        args += list(finish)
        out, out_spec = jax.ShapeDtypeStruct(IMAGE, bf16), whole(IMAGE)
    return pl.pallas_call(
        functools.partial(ffn_kernel, which, last),
        grid=(2, WINDOWS),
        in_specs=in_specs,
        out_specs=[
            whole((2, 2 * BLOCK, D)), pl.BlockSpec((1, 1, BLOCK), lambda j, c: (j, 0, 0)),
            out_spec, late,
        ],
        out_shape=[
            jax.ShapeDtypeStruct((2, 2 * BLOCK, D), bf16),
            jax.ShapeDtypeStruct((2, 1, BLOCK), f32), out, dense(f32),
        ],
        scratch_shapes=[
            pltpu.VMEM((D, BLOCK), f32), pltpu.VMEM((BLOCK, D), f32),
            pltpu.VMEM((WINDOWS, DROWS, D), f32), pltpu.VMEM((WINDOWS, DROWS, D), f32),
            pltpu.VMEM((D, BLOCK), bf16), pltpu.VMEM((BLOCK, D), bf16), VECTORS,
            pltpu.VMEM((1, BLOCK), f32),
        ],
        name="ffn",
        **params(2, 2 * 12 * WINDOWS * DROWS * D * BLOCK, 20e6),
    )(*args)


def run_middle(cot, dh2, mid, att, take, pw, vec):
    drow = by_place(DROWS, D)
    return pl.pallas_call(
        middle_kernel,
        grid=(WINDOWS,),
        in_specs=[
            drow, drow, drow, drow, whole(take.shape), *[whole(pw[0].shape)] * 2,
            *[whole(vec[0].shape)] * 2,
        ],
        out_specs=[drow, by_place(WROWS, D), whole((2, D, D // 2)), whole((8, D))],
        out_shape=[
            dense(f32), jax.ShapeDtypeStruct((WINDOWS, WROWS, D), bf16),
            jax.ShapeDtypeStruct((2, D, D // 2), bf16), jax.ShapeDtypeStruct((8, D), f32),
        ],
        scratch_shapes=[pltpu.VMEM((D, D), f32), pltpu.VMEM((D, D), bf16), VECTORS],
        name="middle_backward",
        **params(1, 3e9, 10e6),
    )(cot, dh2, mid, att, take, *pw, *vec)


def run_heads(part, qkv, prob, dwin, h1, put, hm):
    def columns(at):
        return pl.BlockSpec((None, WROWS, PCOLS), lambda i: (i, 0, at))

    rows = 3 * (D // 2)
    return pl.pallas_call(
        heads_kernel,
        grid=(WINDOWS,),
        in_specs=[
            columns(part), columns(SPLIT + part), columns(2 * SPLIT + part),
            pl.BlockSpec((None, PART, IMGS, WPAD, LANES), lambda i: (i, part, 0, 0, 0)),
            columns(part), by_place(DROWS, D), whole(put.shape), whole(hm.shape),
        ],
        out_specs=[
            by_place(DROWS, 3 * PCOLS), whole((2, rows, D // 2)), whole((8, PCOLS)),
            whole((PART, KEEP, LANES)),
        ],
        out_shape=[
            dense(bf16, 3 * PCOLS), jax.ShapeDtypeStruct((2, rows, D // 2), bf16),
            jax.ShapeDtypeStruct((8, PCOLS), f32),
            jax.ShapeDtypeStruct((PART, KEEP, LANES), f32),
        ],
        scratch_shapes=[
            pltpu.VMEM((WROWS, 3 * PCOLS), bf16), pltpu.VMEM((D, 3 * PCOLS), f32),
        ],
        name="attention_backward",
        **params(1, 4e9, 10e6),
    )(qkv, qkv, qkv, prob, dwin, h1, put, hm)


def run_final(images, dmid, dm0, dm1, qkvw, vec):
    return pl.pallas_call(
        final_kernel,
        grid=(WINDOWS,),
        in_specs=[
            whole(IMAGE), by_place(DROWS, D), by_place(DROWS, 3 * PCOLS),
            by_place(DROWS, 3 * PCOLS), *[whole(qkvw[0].shape)] * 2, *[whole(vec[0].shape)] * 2,
        ],
        out_specs=[whole(IMAGE), whole((8, D))],
        out_shape=[jax.ShapeDtypeStruct(IMAGE, bf16), jax.ShapeDtypeStruct((8, D), f32)],
        scratch_shapes=[pltpu.VMEM((DROWS, D), f32), pltpu.VMEM((D, 3 * D), bf16), VECTORS],
        name="final_backward",
        **params(1, 3e9, 10e6),
    )(images, dmid, dm0, dm1, *qkvw, *vec)


def digits_of(n):
    digits, stride = [], 1
    while n > 1:
        base = 4 if n % 4 == 0 else 2
        digits.append((base, stride))
        stride *= base
        n //= base
    return digits


def make_shards(replicas):
    axes = ("replica", "shard")
    core_pairs = [(r * 2 + s, r * 2 + 1 - s) for r in range(replicas) for s in range(2)]
    digits = digits_of(replicas)

    def across(value):
        return lax.ppermute(value, axes, core_pairs)

    def partner(value, k, stride):
        pairs = [(r * 2 + s, (r ^ (k * stride)) * 2 + s) for r in range(replicas) for s in range(2)]
        return lax.ppermute(value, axes, pairs)

    def place(base, stride):
        return (lax.axis_index("replica") // stride) % base

    def pick(value, index):
        return lax.dynamic_index_in_dim(value, index, 0, keepdims=False)

    def in_order(parts, mine):
        base = len(parts)
        laid = []
        for at in range(base):
            value = parts[at]
            for c in range(1, base):
                value = jnp.where(mine == c, parts[at ^ c], value)
            laid.append(value)
        return jnp.stack(laid)

    def both_halves(value):
        other = across(value)
        first = lax.axis_index("shard") == 0
        return jnp.where(first, value, other), jnp.where(first, other, value)

    def pinned(values, token):
        if token is None:
            return values
        return lax.optimization_barrier((values, token))[0]

    def core_sum(parts):
        s = lax.axis_index("shard")
        send = jnp.concatenate([pick(part, 1 - s) for part in parts], axis=0)
        keep = jnp.concatenate([pick(part, s) for part in parts], axis=0)
        return send, keep, across(send)

    def added(*values):
        total = values[0].astype(f32)
        for value in values[1:]:
            total = total + value.astype(f32)
        return total.astype(bf16)

    def split_sends(buf, base, stride):
        mine = place(base, stride)
        view = buf.reshape(base, buf.shape[0] // base, buf.shape[1])
        return pick(view, mine), [pick(view, mine ^ k) for k in range(1, base)]

    def swap(sends, stride):
        return [partner(value, k + 1, stride) for k, value in enumerate(sends)]

    def two_parts(value):
        top = lax.reduce_precision(value, 8, 7)
        return jnp.concatenate([top.astype(bf16), (value - top).astype(bf16)], axis=0)

    def one_part(rows):
        half = rows.shape[0] // 2
        return rows[:half].astype(f32) + rows[half:].astype(f32)

    def shards(
        images, out_grad, image_counts, regions, relative_index,
        norm1_gain, norm1_bias, qkv_weight, query_bias, value_bias, bias_table,
        proj_weight, proj_bias, norm2_gain, norm2_bias, fc1_weight, fc1_bias, fc2_weight, fc2_bias,
    ):
        shard = lax.axis_index("shard")
        half = D // 2
        images = images.transpose(1, 2, 0, 3)
        out_grad = out_grad.transpose(1, 2, 0, 3)
        qkvw = (qkv_weight, across(qkv_weight))
        vectors = [
            norm1_gain, norm1_bias, query_bias, value_bias,
            proj_bias, norm2_gain, norm2_bias, fc2_bias,
        ] + [fc1_bias[i * half : (i + 1) * half] for i in range(VROWS - FB)]
        at_row = lax.broadcasted_iota(jnp.int32, (VROWS, half), 0)
        packed = jnp.zeros((VROWS, half), bf16)
        for i, value in enumerate(vectors):
            packed = jnp.where(at_row == i, value[None, :], packed)
        vec = (packed, across(packed))
        table = jnp.concatenate(both_halves(bias_table.T), axis=0)
        pw = (proj_weight, across(proj_weight))
        fc1 = (fc1_weight, across(fc1_weight))
        fc2 = (fc2_weight, across(fc2_weight))

        index = jnp.pad(
            relative_index.T, ((0, KEEP - TOKENS), (0, WPAD - TOKENS)), constant_values=-1
        )
        onehot = (
            index.reshape(1, -1) == jnp.arange(TABLE, dtype=jnp.int32)[:, None]
        ).astype(bf16)
        pos = dot(table, onehot).reshape(GROUPS, PACK, KEEP, WPAD)
        pos = pos.transpose(0, 2, 1, 3).reshape(GROUPS, KEEP, LANES)
        labels = regions.reshape(CELLS, WIN, CELLS, WIN).transpose(0, 2, 1, 3)
        labels = labels.reshape(WINDOWS, TOKENS)
        differ = labels[:, :, None] != labels[:, None, :]
        mask = jnp.where(differ, MASK_FILL, 0.0).astype(f32)
        mask = jnp.pad(mask, ((0, 0), (0, 0), (0, WPAD - TOKENS)))
        mask = jnp.pad(mask, ((0, 0), (0, KEEP - TOKENS), (0, 0)), constant_values=PAD_FILL)
        mask = jnp.tile(mask, (1, 1, PACK))

        take_np = window_places()
        take = jnp.asarray(take_np, bf16)
        put = jnp.asarray(take_np.T, bf16)
        hm = jnp.asarray(
            (np.arange(LANES)[:, None] // WPAD) == (np.arange(GCOLS)[None, :] // HEAD), bf16
        )

        qkv, prob, h1, att, mid, h2, cot, cotsum = run_forward(
            images, out_grad, image_counts, take, put, qkvw, pw, vec, pos, mask, hm
        )
        grads_a, fbias_a, oacc, dacc = run_ffn(0, h2, cot, fc1, fc2, vec)
        send, keep, got = core_sum([grads_a])
        h2 = pinned(h2, send)
        grads_b, fbias_b, output, dh2 = run_ffn(1, h2, cot, fc1, fc2, vec, (oacc, dacc, mid))
        keep, got = pinned((keep, got), dh2)
        sum_a = added(keep, got)
        total_a = lax.psum(sum_a, "replica")

        send, keep, got = core_sum([grads_b])
        dh2 = pinned(dh2, (send, sum_a))
        dmid, dwin, gp, small_mid = run_middle(cot, dh2, mid, att, take, pw, vec)
        keep, got = pinned((keep, got), dmid)
        kept, sends = split_sends(added(keep, got), *digits[0])
        gots = swap(sends, digits[0][1])
        dwin = pinned(dwin, sends)
        dm0, grads_c, small_c, bias_c = run_heads(0, qkv, prob, dwin, h1, put, hm)
        kept, gots = pinned((kept, gots), dm0)
        buf_b = added(kept, *gots)
        for base, stride in digits[1:-1]:
            kept, sends = split_sends(buf_b, base, stride)
            buf_b = added(kept, *swap(sends, stride))
        kept, sends = split_sends(buf_b, *digits[-1])
        gots = swap(sends, digits[-1][1])
        dwin = pinned(dwin, sends)
        dm1, grads_d, small_d, bias_d = run_heads(1, qkv, prob, dwin, h1, put, hm)

        send, keep, got = core_sum([grads_c, gp, grads_d])
        kept, gots = pinned((kept, gots), dm1)
        buf_b = added(kept, *gots)
        gots_b = swap([buf_b] * (digits[-1][0] - 1), digits[-1][1])
        kept, sends = split_sends(added(keep, got), *digits[0])
        gots = swap(sends, digits[0][1])
        dm1 = pinned(dm1, (sends, buf_b))
        grad_images, small_end = run_final(images, dmid, dm0, dm1, qkvw, vec)
        kept, gots, buf_b, gots_b = pinned((kept, gots, buf_b, gots_b), small_end)

        bias_sum = jnp.concatenate([bias_c, bias_d], axis=0)
        by_head = bias_sum.reshape(GROUPS, KEEP, PACK, WPAD).transpose(0, 2, 1, 3)
        table_grad = lax.dot_general(
            by_head.reshape(HEADS, -1), onehot.astype(f32), (((1,), (1,)), ((), ())),
            precision=HIGH, preferred_element_type=f32,
        )
        table_rows = jnp.pad(table_grad, ((0, 0), (0, half - TABLE)))
        fbias = [fbias_a[0], fbias_b[0], fbias_a[1], fbias_b[1]]
        rows = jnp.concatenate([small_end[0:2], small_mid[0:3], cotsum, *fbias], axis=0)
        small = jnp.concatenate(
            [rows[:, :half], rows[:, half:], small_c[0:2], small_d[0:2], table_rows], axis=0
        )

        buf = added(kept, *gots)
        for base, stride in digits[1:]:
            kept, sends = split_sends(buf, base, stride)
            extra = two_parts(small)
            cut = kept.shape[0]
            gots = swap([jnp.concatenate([value, extra], axis=0) for value in sends], stride)
            buf = added(kept, *[value[:cut] for value in gots])
            for value in gots:
                small = small + one_part(value[cut:])

        def back(buf, gots, base, stride):
            return in_order([buf] + gots, place(base, stride)).reshape(-1, buf.shape[1])

        buf_b = back(buf_b, gots_b, *digits[-1])
        for base, stride in reversed(digits[:-1]):
            buf_b = back(buf_b, swap([buf_b] * (base - 1), stride), base, stride)
        for base, stride in reversed(digits[1:]):
            buf = back(buf, swap([buf] * (base - 1), stride), base, stride)
        base, stride = digits[0]
        cut = buf.shape[0]
        extra = two_parts(small)
        gots = swap([jnp.concatenate([buf, extra], axis=0)] * (base - 1), stride)
        buf = back(buf, [value[:cut] for value in gots], base, stride)
        for value in gots:
            small = small + one_part(value[cut:])
        small = small + across(small)
        total_a = pinned(total_a, buf)
        sum_a, sum_b, sum_c = total_a.astype(f32), buf_b.astype(f32), buf.astype(f32)

        n = 2 + 3 + 1 + 4
        mine = lax.dynamic_slice(small, (shard * n, 0), (n, half))
        sides = small[2 * n : 2 * n + 4]
        query_sum, value_sum = [
            lax.dynamic_index_in_dim(sides[i::2], shard, 0, keepdims=False) for i in range(2)
        ]
        own_table = lax.dynamic_slice(
            small, (2 * n + 4 + shard * (HEADS // 2), 0), (HEADS // 2, half)
        )[:, :TABLE].T
        fsum = small[: 2 * n].reshape(2, n, half)[:, 6:]
        own_fb = lax.dynamic_slice(fsum, (0, 2 * shard, 0), (2, 2, half))
        own_fb = own_fb.transpose(1, 0, 2).reshape(-1)
        grad_fc2 = jnp.concatenate([sum_a[:BLOCK], sum_b[:BLOCK]], axis=0)
        grad_fc1 = jnp.concatenate(
            [sum_a[BLOCK : BLOCK + half], sum_b[BLOCK : BLOCK + half],
             sum_a[BLOCK + half :], sum_b[BLOCK + half :]], axis=1,
        )
        start = 3 * half + D
        grad_qkv = jnp.concatenate(
            [sum_c[at + b * half : at + (b + 1) * half] for b in range(3) for at in (0, start)],
            axis=1,
        )
        grad_proj = jnp.concatenate(
            [sum_c[3 * half : 4 * half], sum_c[4 * half : 5 * half]], axis=1
        )
        return (
            output.transpose(2, 0, 1, 3), grad_images.transpose(2, 0, 1, 3),
            mine[0], mine[1], grad_qkv, query_sum, value_sum, own_table,
            grad_proj, mine[4], mine[2], mine[3], grad_fc1, own_fb, grad_fc2, mine[5],
        )

    return shards


def solution(mesh):
    return jax.shard_map(
        make_shards(mesh.shape["replica"]),
        mesh=mesh,
        in_specs=(
            P(("replica", "shard"), None, None, None),
            P(("replica", "shard"), None, None, None),
            P(("replica", "shard")),
            P(),
            P(),
            P("shard"),
            P("shard"),
            P("shard", None),
            P("shard"),
            P("shard"),
            P(None, "shard"),
            P("shard", None),
            P("shard"),
            P("shard"),
            P("shard"),
            P("shard", None),
            P("shard"),
            P("shard", None),
            P("shard"),
        ),
        out_specs=(
            P(("replica", "shard"), None, None, None),
            P(("replica", "shard"), None, None, None),
            P("shard"),
            P("shard"),
            P("shard", None),
            P("shard"),
            P("shard"),
            P(None, "shard"),
            P("shard", None),
            P("shard"),
            P("shard"),
            P("shard"),
            P("shard", None),
            P("shard"),
            P("shard", None),
            P("shard"),
        ),
        check_vma=False,
    )
```

```python
import functools

import jax
import jax.numpy as jnp
import numpy as np
from jax import lax
from jax.experimental import pallas as pl
from jax.experimental.pallas import tpu as pltpu
from jax.sharding import PartitionSpec as P

D = 512
HEADS = 16
HEAD = 32
FF = 2048
SIDE = 14
WIN = 7
SHIFT = 3
TABLE = 169
EPSILON = 1e-05
MASK_FILL = -100.0
PAD_FILL = -1e30
SCALE = HEAD**-0.5
HIGH = lax.Precision.HIGHEST

TOKENS = WIN * WIN
CELLS = SIDE // WIN
WINDOWS = CELLS**2
IMGS = 8
WPAD = 64
WROWS = IMGS * WPAD
DROWS = TOKENS * IMGS
PACK = 4
GROUPS = HEADS // PACK
GCOLS = PACK * HEAD
LANES = PACK * WPAD
SPLIT = 2
PART = GROUPS // SPLIT
PCOLS = PART * GCOLS
BLOCK = 512
BATCH = 16
KEEP = 56

f32 = jnp.float32
bf16 = jnp.bfloat16


def window_places():
    take = np.zeros((WROWS, DROWS), np.float32)
    for i in range(IMGS):
        for t in range(TOKENS):
            take[i * WPAD + t, t * IMGS + i] = 1
    return take


def dot(a, b):
    return lax.dot_general(a, b, (((1,), (0,)), ((), ())), preferred_element_type=f32)


def dot_nt(a, b):
    return lax.dot_general(a, b, (((1,), (1,)), ((), ())), preferred_element_type=f32)


def dot_tn(a, b):
    return lax.dot_general(a, b, (((0,), (0,)), ((), ())), preferred_element_type=f32)


def normed(x):
    centred = x - jnp.mean(x, axis=-1, keepdims=True)
    rstd = lax.rsqrt(jnp.mean(centred * centred, axis=-1, keepdims=True) + EPSILON)
    return centred * rstd, rstd


def norm_back(grad, gain, hat, rstd):
    g = grad * gain
    mean_g = jnp.mean(g, axis=-1, keepdims=True)
    mean_gh = jnp.mean(g * hat, axis=-1, keepdims=True)
    return rstd * (g - mean_g - hat * mean_gh)


def spread_heads(block, head_mask):
    return jnp.concatenate([block] * PACK, axis=0) * head_mask


def gather_heads(result):
    lane = lax.broadcasted_iota(jnp.int32, (WPAD, GCOLS), 1) // HEAD
    parts = [result[h * WPAD : (h + 1) * WPAD] for h in range(PACK)]
    out = parts[PACK - 1]
    for h in range(PACK - 2, -1, -1):
        out = jnp.where(lane == h, parts[h], out)
    return out


def token_places(place):
    row0 = (place // CELLS) * WIN + SHIFT
    col0 = (place % CELLS) * WIN + SHIFT
    for i in range(WIN):
        r = row0 + i
        r = jnp.where(r >= SIDE, r - SIDE, r)
        for j in range(WIN):
            c = col0 + j
            yield (i * WIN + j) * IMGS, r, jnp.where(c >= SIDE, c - SIDE, c)


def load_window(rows, ref, place):
    for at, r, c in token_places(place):
        rows[at : at + IMGS] = ref[r, c].astype(f32)
    return rows[...]


def store_window(ref, value, place):
    for at, r, c in token_places(place):
        ref[r, c] = value[at : at + IMGS].astype(bf16)


def join_rows(full, own_ref, other_ref):
    half = full.shape[0] // 2
    first = lax.axis_index("shard") == 0

    @pl.when(first)
    def _():
        full[0:half] = own_ref[...]
        full[half:] = other_ref[...]

    @pl.when(jnp.logical_not(first))
    def _():
        full[0:half] = other_ref[...]
        full[half:] = own_ref[...]


def join_vectors(vec, own_ref, other_ref):
    first = lax.axis_index("shard") == 0
    own, other = own_ref[...].astype(f32), other_ref[...].astype(f32)
    vec[:, 0 : D // 2] = jnp.where(first, own, other)
    vec[:, D // 2 :] = jnp.where(first, other, own)


G1, B1, QB, VB, PB, G2, B2, F2B, FB = range(9)
VROWS = 12


def forward_kernel(
    count_ref, img_ref, og_ref, take_ref, put_ref, qw0_ref, qw1_ref, pw0_ref, pw1_ref,
    vec0_ref, vec1_ref, pos_ref, mask_ref, hm_ref,
    qkv_out, prob_out, h1_out, att_out, mid_out, h2_out, cot_out, cotsum_out,
    rows_in, att, qkvw_ref, pw_ref, vec,
):
    place = pl.program_id(0)

    @pl.when(place == 0)
    def _():
        cotsum_out[...] = jnp.zeros_like(cotsum_out)
        join_rows(qkvw_ref, qw0_ref, qw1_ref)
        join_rows(pw_ref, pw0_ref, pw1_ref)
        join_vectors(vec, vec0_ref, vec1_ref)

    def row(at):
        return vec[at : at + 1]

    image = lax.broadcasted_iota(jnp.int32, (DROWS, D), 0) % IMGS
    cot = jnp.where(image < count_ref[0], load_window(rows_in, og_ref, place), 0.0)
    cot_out[...] = cot.astype(bf16)
    cotsum_out[...] += jnp.sum(cot, axis=0, keepdims=True)

    x = load_window(rows_in, img_ref, place)
    hat, _ = normed(x)
    h1 = (hat * row(G1) + row(B1)).astype(bf16)
    h1_out[...] = h1
    tiles = dot(take_ref[...], h1).astype(bf16)
    qkv_out[:, 0:D] = (dot(tiles, qkvw_ref[:, 0:D]) + row(QB)).astype(bf16)
    qkv_out[:, D : 2 * D] = dot(tiles, qkvw_ref[:, D : 2 * D]).astype(bf16)
    qkv_out[:, 2 * D : 3 * D] = (dot(tiles, qkvw_ref[:, 2 * D : 3 * D]) + row(VB)).astype(bf16)
    head_mask = hm_ref[...]
    units = [(i, g) for g in range(GROUPS) for i in range(IMGS)]
    for at in range(0, len(units), BATCH):
        batch = units[at : at + BATCH]
        rows = [slice(i * WPAD, (i + 1) * WPAD) for i, _ in batch]
        cols = [slice(g * GCOLS, (g + 1) * GCOLS) for _, g in batch]
        wide = [spread_heads(qkv_out[r, c], head_mask) for r, c in zip(rows, cols)]
        keys = [qkv_out[r, D + c.start : D + c.stop] for r, c in zip(rows, cols)]
        s = [dot_nt(k, q)[:KEEP] for k, q in zip(keys, wide)]
        s = [v * SCALE + pos_ref[g] + mask_ref[...] for v, (_, g) in zip(s, batch)]
        e = [jnp.exp(v - jnp.max(v, axis=0, keepdims=True)) for v in s]
        p = [v / jnp.sum(v, axis=0, keepdims=True) for v in e]
        zero = jnp.zeros((WPAD - KEEP, LANES), f32)
        p = [jnp.concatenate([v, zero], axis=0).astype(bf16) for v in p]
        for v, (i, g) in zip(p, batch):
            prob_out[g, i] = v
        values = [qkv_out[r, 2 * D + c.start : 2 * D + c.stop] for r, c in zip(rows, cols)]
        found = [dot_tn(v, w) for v, w in zip(p, values)]
        for r, c, v in zip(rows, cols, found):
            att[r, c] = gather_heads(v).astype(bf16)
    a = dot(put_ref[...], att[...]).astype(bf16)
    att_out[...] = a
    middle = x + (dot(a, pw_ref[...]) + row(PB))
    mid_out[...] = middle
    hat2, _ = normed(middle)
    h2_out[...] = (hat2 * row(G2) + row(B2)).astype(bf16)


def ffn_kernel(which, last, *refs):
    refs = list(refs)
    h2_ref, cot_ref, f10_ref, f11_ref, f20_ref, f21_ref, vec0_ref, vec1_ref = refs[:8]
    refs = refs[8:]
    if last:
        oin_ref, din_ref, mid_ref = refs[:3]
        refs = refs[3:]
    grads, bias_out, out_ref, dh2_ref, acc1, acc2, oacc, dacc, f1_ref, f2_ref, vec, fbias = refs
    j, c = pl.program_id(0), pl.program_id(1)

    @pl.when(c == 0)
    def _():
        mine = lax.axis_index("shard") == j
        join_rows(f1_ref, f10_ref, f11_ref)
        join_vectors(vec, vec0_ref, vec1_ref)

        def owner_parts(f2, vectors):
            f2_ref[...] = f2[...]
            for b in range(BLOCK // (D // 2)):
                at = FB + which * (BLOCK // (D // 2)) + b
                fbias[:, b * D // 2 : (b + 1) * D // 2] = vectors[at : at + 1].astype(f32)

        @pl.when(mine)
        def _():
            owner_parts(f20_ref, vec0_ref)

        @pl.when(jnp.logical_not(mine))
        def _():
            owner_parts(f21_ref, vec1_ref)

    h2 = h2_ref[...]
    cot = cot_ref[...]
    hidden = dot(h2, f1_ref[...]) + fbias[...]
    dact = dot_nt(cot, f2_ref[...])
    bell = jnp.exp(hidden * hidden * -0.5)
    base = 1.0 + jnp.abs(hidden) * (0.3275911 * 0.5**0.5)
    t = pl.reciprocal(base, approx=True)
    t = t * (2.0 - base * t)
    half = t * (
        0.127414796
        + t * (-0.142248368 + t * (0.7107068705 + t * (-0.7265760135 + t * 0.5307027145)))
    )
    half = half * bell
    phi = jnp.where(hidden > 0, 1.0 - half, half)
    act = (hidden * phi).astype(bf16)
    dhid = dact * (phi + hidden * bell * 0.3989422804014327)
    dhid_low = dhid.astype(bf16)

    g2 = dot_tn(act, cot)
    g1 = dot_tn(h2, dhid_low)
    fb = jnp.sum(dhid, axis=0, keepdims=True)
    o = dot(act, f2_ref[...])
    d = dot_nt(dhid_low, f1_ref[...])

    acc1[...] = jnp.where(c == 0, 0.0, acc1[...]) + g1
    acc2[...] = jnp.where(c == 0, 0.0, acc2[...]) + g2
    bias_out[0] = jnp.where(c == 0, 0.0, bias_out[0]) + fb
    o = jnp.where(j == 0, 0.0, oacc[c]) + o
    d = jnp.where(j == 0, 0.0, dacc[c]) + d
    oacc[c] = o
    dacc[c] = d
    if last:
        dh2_ref[...] = d + din_ref[...]
        store_window(out_ref, mid_ref[...] + (o + oin_ref[...]) + vec[F2B : F2B + 1], c)
    else:
        dh2_ref[...] = d
        out_ref[...] = o

    half_rows = D // 2

    @pl.when(c == pl.num_programs(1) - 1)
    def _():
        grads[j, 0:BLOCK] = acc2[...].astype(bf16)
        place = pl.ds(pl.multiple_of(BLOCK + j * half_rows, half_rows), half_rows)
        grads[0, place] = acc1[0:half_rows].astype(bf16)
        grads[1, place] = acc1[half_rows:D].astype(bf16)


def middle_kernel(
    cot_ref, dh2_ref, mid_ref, att_ref, take_ref, pw0_ref, pw1_ref, vec0_ref, vec1_ref,
    dmid_out, dwin_out, grads, small, gp, pw_ref, vec,
):
    place = pl.program_id(0)

    @pl.when(place == 0)
    def _():
        small[...] = jnp.zeros_like(small)
        gp[...] = jnp.zeros_like(gp)
        join_rows(pw_ref, pw0_ref, pw1_ref)
        join_vectors(vec, vec0_ref, vec1_ref)

    hat2, rstd2 = normed(mid_ref[...])
    dh2 = dh2_ref[...]
    small[0:1] += jnp.sum(dh2 * hat2, axis=0, keepdims=True)
    small[1:2] += jnp.sum(dh2, axis=0, keepdims=True)
    dmid = cot_ref[...].astype(f32) + norm_back(dh2, vec[G2 : G2 + 1], hat2, rstd2)
    small[2:3] += jnp.sum(dmid, axis=0, keepdims=True)
    dmid_out[...] = dmid
    dbr = dmid.astype(bf16)
    gp[...] += dot_tn(att_ref[...], dbr)
    datt = dot_nt(dbr, pw_ref[...]).astype(bf16)
    dwin_out[...] = dot(take_ref[...], datt).astype(bf16)

    @pl.when(place == pl.num_programs(0) - 1)
    def _():
        half = D // 2
        for o in range(2):
            for b in range(2):
                grads[o, b * half : (b + 1) * half] = gp[
                    o * half : (o + 1) * half, b * half : (b + 1) * half
                ].astype(bf16)


def heads_kernel(
    q_ref, k_ref, v_ref, prob_ref, dwin_ref, h1_ref, put_ref, hm_ref,
    dm_out, grads, small, bias_out, dmix, gq,
):
    place = pl.program_id(0)

    @pl.when(place == 0)
    def _():
        small[...] = jnp.zeros_like(small)
        bias_out[...] = jnp.zeros_like(bias_out)
        gq[...] = jnp.zeros_like(gq)

    head_mask = hm_ref[...]
    units = [(i, g) for g in range(PART) for i in range(IMGS)]
    zero = jnp.zeros((WPAD - KEEP, LANES), f32)
    for at in range(0, len(units), BATCH):
        batch = units[at : at + BATCH]
        rows = [slice(i * WPAD, (i + 1) * WPAD) for i, _ in batch]
        cols = [slice(g * GCOLS, (g + 1) * GCOLS) for _, g in batch]
        wide = [spread_heads(dwin_ref[r, c], head_mask) for r, c in zip(rows, cols)]
        dp = [dot_nt(v_ref[r, c], da)[:KEEP] for r, c, da in zip(rows, cols, wide)]
        low = [prob_ref[g, i] for i, g in batch]
        dv = [dot(p, da) for p, da in zip(low, wide)]
        p = [v.astype(f32)[:KEEP] for v in low]
        inner = [jnp.sum(x * y, axis=0, keepdims=True) for x, y in zip(dp, p)]
        ds = [(y * (x - n)).astype(bf16).astype(f32) for x, y, n in zip(dp, p, inner)]
        for v, (_, g) in zip(ds, batch):
            bias_out[g] += v
        ds = [jnp.concatenate([v, zero], axis=0).astype(bf16) for v in ds]
        dq = [dot_tn(v, k_ref[r, c]) for v, r, c in zip(ds, rows, cols)]
        queries = [spread_heads(q_ref[r, c], head_mask) for r, c in zip(rows, cols)]
        dk = [dot(v, q) for v, q in zip(ds, queries)]
        for r, c, x, y, w in zip(rows, cols, dq, dk, dv):
            dmix[r, c] = (gather_heads(x) * SCALE).astype(bf16)
            dmix[r, PCOLS + c.start : PCOLS + c.stop] = (y * SCALE).astype(bf16)
            dmix[r, 2 * PCOLS + c.start : 2 * PCOLS + c.stop] = w.astype(bf16)
    small[0:1] += jnp.sum(dmix[:, 0:PCOLS].astype(f32), axis=0, keepdims=True)
    small[1:2] += jnp.sum(dmix[:, 2 * PCOLS : 3 * PCOLS].astype(f32), axis=0, keepdims=True)
    dm = dot(put_ref[...], dmix[...]).astype(bf16)
    dm_out[...] = dm
    gq[...] += dot_tn(h1_ref[...], dm)

    @pl.when(place == pl.num_programs(0) - 1)
    def _():
        half = D // 2
        for o in range(2):
            for b in range(3):
                grads[o, b * half : (b + 1) * half] = gq[
                    o * half : (o + 1) * half, b * PCOLS : (b + 1) * PCOLS
                ].astype(bf16)


def final_kernel(
    img_ref, dmid_ref, dm0_ref, dm1_ref, qw0_ref, qw1_ref, vec0_ref, vec1_ref,
    out_ref, small, rows_in, qkvw_ref, vec,
):
    place = pl.program_id(0)

    @pl.when(place == 0)
    def _():
        small[...] = jnp.zeros_like(small)
        join_rows(qkvw_ref, qw0_ref, qw1_ref)
        join_vectors(vec, vec0_ref, vec1_ref)

    dh1 = None
    for part, ref in enumerate((dm0_ref, dm1_ref)):
        for b in range(3):
            at = b * D + part * PCOLS
            term = dot_nt(ref[:, b * PCOLS : (b + 1) * PCOLS], qkvw_ref[:, at : at + PCOLS])
            dh1 = term if dh1 is None else dh1 + term
    hat1, rstd1 = normed(load_window(rows_in, img_ref, place))
    small[0:1] += jnp.sum(dh1 * hat1, axis=0, keepdims=True)
    small[1:2] += jnp.sum(dh1, axis=0, keepdims=True)
    store_window(out_ref, dmid_ref[...] + norm_back(dh1, vec[G1 : G1 + 1], hat1, rstd1), place)


def far(value):
    return pltpu.with_memory_space_constraint(value, pltpu.HBM)


def all_far(values):
    return [far(value) for value in values]


def whole(shape):
    return pl.BlockSpec(shape, lambda *_: (0,) * len(shape))


def by_place(*dims):
    return pl.BlockSpec((None,) + dims, lambda i: (i,) + (0,) * len(dims))


def params(axes, flops, size):
    return dict(
        compiler_params=pltpu.CompilerParams(
            dimension_semantics=("arbitrary",) * axes, vmem_limit_bytes=24 * 1024 * 1024
        ),
        cost_estimate=pl.CostEstimate(flops=int(flops), bytes_accessed=int(size), transcendentals=0),
    )


IMAGE = (SIDE, SIDE, IMGS, D)


def dense(kind, cols=D):
    return jax.ShapeDtypeStruct((WINDOWS, DROWS, cols), kind)


VECTORS = pltpu.VMEM((VROWS, D), f32)


def run_forward(images, out_grad, count, take, put, qkvw, pw, vec, pos, mask, hm):
    drow = by_place(DROWS, D)
    pair = [whole(qkvw[0].shape)] * 2 + [whole(pw[0].shape)] * 2 + [whole(vec[0].shape)] * 2
    return pl.pallas_call(
        forward_kernel,
        grid=(WINDOWS,),
        in_specs=[
            pl.BlockSpec(memory_space=pltpu.SMEM), whole(IMAGE), whole(IMAGE),
            whole(take.shape), whole(put.shape), *pair,
            whole(pos.shape), by_place(KEEP, LANES), whole(hm.shape),
        ],
        out_specs=[
            by_place(WROWS, 3 * D), by_place(GROUPS, IMGS, WPAD, LANES),
            drow, drow, drow, drow, drow, whole((1, D)),
        ],
        out_shape=[
            pltpu.HBM((WINDOWS, WROWS, 3 * D), bf16),
            pltpu.HBM((WINDOWS, GROUPS, IMGS, WPAD, LANES), bf16),
            pltpu.HBM((WINDOWS, DROWS, D), bf16), pltpu.HBM((WINDOWS, DROWS, D), bf16),
            pltpu.HBM((WINDOWS, DROWS, D), f32), dense(bf16), dense(bf16),
            jax.ShapeDtypeStruct((1, D), f32),
        ],
        scratch_shapes=[
            pltpu.VMEM((DROWS, D), f32), pltpu.VMEM((WROWS, D), bf16),
            pltpu.VMEM((D, 3 * D), bf16), pltpu.VMEM((D, D), bf16), VECTORS,
        ],
        name="forward_attention",
        **params(1, 9e9, 25e6),
    )(count, *all_far([images, out_grad, take, put, *qkvw, *pw, *vec, pos, mask, hm]))


def run_ffn(which, h2, cot, fc1, fc2, vec, finish=None):
    last = finish is not None
    chunk = pl.BlockSpec((None, DROWS, D), lambda j, c: (c, 0, 0))
    late = pl.BlockSpec((None, DROWS, D), lambda j, c: (c * j, 0, 0))
    f1 = pl.BlockSpec((D // 2, BLOCK), lambda j, c: (0, 2 * j + which))
    f2 = pl.BlockSpec((BLOCK, D), lambda j, c: (which, 0))
    vecs = whole(vec[0].shape)
    in_specs = [chunk, chunk, f1, f1, f2, f2, vecs, vecs]
    args = [h2, cot, *all_far([*fc1, *fc2, *vec])]
    out, out_spec = pltpu.HBM((WINDOWS, DROWS, D), f32), late
    if last:
        in_specs += [late, late, late]
        args += all_far(finish)
        out, out_spec = jax.ShapeDtypeStruct(IMAGE, bf16), whole(IMAGE)
    return pl.pallas_call(
        functools.partial(ffn_kernel, which, last),
        grid=(2, WINDOWS),
        in_specs=in_specs,
        out_specs=[
            whole((2, 2 * BLOCK, D)), pl.BlockSpec((1, 1, BLOCK), lambda j, c: (j, 0, 0)),
            out_spec, late,
        ],
        out_shape=[
            jax.ShapeDtypeStruct((2, 2 * BLOCK, D), bf16),
            jax.ShapeDtypeStruct((2, 1, BLOCK), f32), out,
            dense(f32) if last else pltpu.HBM((WINDOWS, DROWS, D), f32),
        ],
        scratch_shapes=[
            pltpu.VMEM((D, BLOCK), f32), pltpu.VMEM((BLOCK, D), f32),
            pltpu.VMEM((WINDOWS, DROWS, D), f32), pltpu.VMEM((WINDOWS, DROWS, D), f32),
            pltpu.VMEM((D, BLOCK), bf16), pltpu.VMEM((BLOCK, D), bf16), VECTORS,
            pltpu.VMEM((1, BLOCK), f32),
        ],
        name="ffn",
        **params(2, 2 * 12 * WINDOWS * DROWS * D * BLOCK, 20e6),
    )(*args)


def run_middle(cot, dh2, mid, att, take, pw, vec):
    drow = by_place(DROWS, D)
    return pl.pallas_call(
        middle_kernel,
        grid=(WINDOWS,),
        in_specs=[
            drow, drow, drow, drow, whole(take.shape), *[whole(pw[0].shape)] * 2,
            *[whole(vec[0].shape)] * 2,
        ],
        out_specs=[drow, by_place(WROWS, D), whole((2, D, D // 2)), whole((8, D))],
        out_shape=[
            dense(f32), jax.ShapeDtypeStruct((WINDOWS, WROWS, D), bf16),
            jax.ShapeDtypeStruct((2, D, D // 2), bf16), jax.ShapeDtypeStruct((8, D), f32),
        ],
        scratch_shapes=[pltpu.VMEM((D, D), f32), pltpu.VMEM((D, D), bf16), VECTORS],
        name="middle_backward",
        **params(1, 3e9, 10e6),
    )(cot, dh2, *all_far([mid, att, take, *pw, *vec]))


def run_heads(part, qkv, prob, dwin, h1, put, hm):
    def columns(at):
        return pl.BlockSpec((None, WROWS, PCOLS), lambda i: (i, 0, at))

    rows = 3 * (D // 2)
    return pl.pallas_call(
        heads_kernel,
        grid=(WINDOWS,),
        in_specs=[
            columns(part), columns(SPLIT + part), columns(2 * SPLIT + part),
            pl.BlockSpec((None, PART, IMGS, WPAD, LANES), lambda i: (i, part, 0, 0, 0)),
            columns(part), by_place(DROWS, D), whole(put.shape), whole(hm.shape),
        ],
        out_specs=[
            by_place(DROWS, 3 * PCOLS), whole((2, rows, D // 2)), whole((8, PCOLS)),
            whole((PART, KEEP, LANES)),
        ],
        out_shape=[
            dense(bf16, 3 * PCOLS), jax.ShapeDtypeStruct((2, rows, D // 2), bf16),
            jax.ShapeDtypeStruct((8, PCOLS), f32),
            jax.ShapeDtypeStruct((PART, KEEP, LANES), f32),
        ],
        scratch_shapes=[
            pltpu.VMEM((WROWS, 3 * PCOLS), bf16), pltpu.VMEM((D, 3 * PCOLS), f32),
        ],
        name="attention_backward",
        **params(1, 4e9, 10e6),
    )(*all_far([qkv, qkv, qkv, prob]), dwin, *all_far([h1, put, hm]))


def run_final(images, dmid, dm0, dm1, qkvw, vec):
    return pl.pallas_call(
        final_kernel,
        grid=(WINDOWS,),
        in_specs=[
            whole(IMAGE), by_place(DROWS, D), by_place(DROWS, 3 * PCOLS),
            by_place(DROWS, 3 * PCOLS), *[whole(qkvw[0].shape)] * 2, *[whole(vec[0].shape)] * 2,
        ],
        out_specs=[whole(IMAGE), whole((8, D))],
        out_shape=[jax.ShapeDtypeStruct(IMAGE, bf16), jax.ShapeDtypeStruct((8, D), f32)],
        scratch_shapes=[pltpu.VMEM((DROWS, D), f32), pltpu.VMEM((D, 3 * D), bf16), VECTORS],
        name="final_backward",
        **params(1, 3e9, 10e6),
    )(far(images), dmid, dm0, dm1, *all_far([*qkvw, *vec]))


def digits_of(n):
    digits, stride = [], 1
    while n > 1:
        base = 4 if n % 4 == 0 else 2
        digits.append((base, stride))
        stride *= base
        n //= base
    return digits


def make_shards(replicas):
    axes = ("replica", "shard")
    core_pairs = [(r * 2 + s, r * 2 + 1 - s) for r in range(replicas) for s in range(2)]
    digits = digits_of(replicas)

    def across(value):
        return lax.ppermute(value, axes, core_pairs)

    def partner(value, k, stride):
        pairs = [(r * 2 + s, (r ^ (k * stride)) * 2 + s) for r in range(replicas) for s in range(2)]
        return lax.ppermute(value, axes, pairs)

    def place(base, stride):
        return (lax.axis_index("replica") // stride) % base

    def pick(value, index):
        return lax.dynamic_index_in_dim(value, index, 0, keepdims=False)

    def in_order(parts, mine):
        base = len(parts)
        laid = []
        for at in range(base):
            value = parts[at]
            for c in range(1, base):
                value = jnp.where(mine == c, parts[at ^ c], value)
            laid.append(value)
        return jnp.stack(laid)

    def both_halves(value):
        other = across(value)
        first = lax.axis_index("shard") == 0
        return jnp.where(first, value, other), jnp.where(first, other, value)

    def tie(*values):
        return lax.optimization_barrier(values)

    def core_halves(parts):
        s = lax.axis_index("shard")
        return [
            jnp.concatenate([pick(part, at) for part in parts], axis=0) for at in (1 - s, s)
        ]

    def added(*values):
        total = values[0].astype(f32)
        for value in values[1:]:
            total = total + value.astype(f32)
        return total.astype(bf16)

    def split_sends(buf, base, stride):
        mine = place(base, stride)
        view = buf.reshape(base, buf.shape[0] // base, buf.shape[1])
        return pick(view, mine), [pick(view, mine ^ k) for k in range(1, base)]

    def swap(sends, stride):
        return [partner(value, k + 1, stride) for k, value in enumerate(sends)]

    def two_parts(value):
        top = lax.reduce_precision(value, 8, 7)
        return jnp.concatenate([top.astype(bf16), (value - top).astype(bf16)], axis=0)

    def one_part(rows):
        half = rows.shape[0] // 2
        return rows[:half].astype(f32) + rows[half:].astype(f32)

    def shards(
        images, out_grad, image_counts, regions, relative_index,
        norm1_gain, norm1_bias, qkv_weight, query_bias, value_bias, bias_table,
        proj_weight, proj_bias, norm2_gain, norm2_bias, fc1_weight, fc1_bias, fc2_weight, fc2_bias,
    ):
        shard = lax.axis_index("shard")
        half = D // 2
        images = images.transpose(1, 2, 0, 3)
        out_grad = out_grad.transpose(1, 2, 0, 3)
        qkvw = (qkv_weight, across(qkv_weight))
        vectors = [
            norm1_gain, norm1_bias, query_bias, value_bias,
            proj_bias, norm2_gain, norm2_bias, fc2_bias,
        ] + [fc1_bias[i * half : (i + 1) * half] for i in range(VROWS - FB)]
        at_row = lax.broadcasted_iota(jnp.int32, (VROWS, half), 0)
        packed = jnp.zeros((VROWS, half), bf16)
        for i, value in enumerate(vectors):
            packed = jnp.where(at_row == i, value[None, :], packed)
        vec = (packed, across(packed))
        table = jnp.concatenate(both_halves(bias_table.T), axis=0)
        pw = (proj_weight, across(proj_weight))
        fc1 = (fc1_weight, across(fc1_weight))
        fc2 = (fc2_weight, across(fc2_weight))

        index = jnp.pad(
            relative_index.T, ((0, KEEP - TOKENS), (0, WPAD - TOKENS)), constant_values=-1
        )
        onehot = (
            index.reshape(1, -1) == jnp.arange(TABLE, dtype=jnp.int32)[:, None]
        ).astype(bf16)
        pos = dot(table, onehot).reshape(GROUPS, PACK, KEEP, WPAD)
        pos = pos.transpose(0, 2, 1, 3).reshape(GROUPS, KEEP, LANES)
        labels = regions.reshape(CELLS, WIN, CELLS, WIN).transpose(0, 2, 1, 3)
        labels = labels.reshape(WINDOWS, TOKENS)
        differ = labels[:, :, None] != labels[:, None, :]
        mask = jnp.where(differ, MASK_FILL, 0.0).astype(f32)
        mask = jnp.pad(mask, ((0, 0), (0, 0), (0, WPAD - TOKENS)))
        mask = jnp.pad(mask, ((0, 0), (0, KEEP - TOKENS), (0, 0)), constant_values=PAD_FILL)
        mask = jnp.tile(mask, (1, 1, PACK))

        take_np = window_places()
        take = jnp.asarray(take_np, bf16)
        put = jnp.asarray(take_np.T, bf16)
        hm = jnp.asarray(
            (np.arange(LANES)[:, None] // WPAD) == (np.arange(GCOLS)[None, :] // HEAD), bf16
        )

        qkv, prob, h1, att, mid, h2, cot, cotsum = run_forward(
            images, out_grad, image_counts, take, put, qkvw, pw, vec, pos, mask, hm
        )
        near, wide = digits[0], digits[-1]

        def inner(buf):
            for base, stride in digits[1:-1]:
                kept, sends = split_sends(buf, base, stride)
                buf = added(kept, *swap(sends, stride))
            return buf

        def back(buf, gots, base, stride):
            return in_order([buf] + gots, place(base, stride)).reshape(-1, buf.shape[1])

        def inner_back(buf):
            for base, stride in reversed(digits[1:-1]):
                buf = back(buf, swap([buf] * (base - 1), stride), base, stride)
            return buf

        def spread(buf, base, stride):
            return swap([buf] * (base - 1), stride)

        grads_a, fbias_a, oacc, dacc = run_ffn(0, h2, cot, fc1, fc2, vec)
        send, keep = core_halves([grads_a])
        kept_a, sends_a = split_sends(added(keep, across(send)), *near)
        kept_a, sends_a, h2 = tie(kept_a, sends_a, h2)
        gots_a = swap(sends_a, near[1])

        grads_b, fbias_b, output, dh2 = run_ffn(1, h2, cot, fc1, fc2, vec, (oacc, dacc, mid))
        send, keep = core_halves([grads_b])
        kept_a, gots_a, send, keep, dh2 = tie(kept_a, gots_a, send, keep, dh2)
        got = across(send)
        kept_a, sends_a = split_sends(inner(added(kept_a, *gots_a)), *wide)
        kept_a, sends_a, dh2 = tie(kept_a, sends_a, dh2)
        gots_a = swap(sends_a, wide[1])

        dmid, dwin, gp, small_mid = run_middle(cot, dh2, mid, att, take, pw, vec)
        kept_a, gots_a, keep, got, dwin = tie(kept_a, gots_a, keep, got, dwin)
        kept_b, sends_b = split_sends(added(keep, got), *near)
        buf_a = added(kept_a, *gots_a)
        buf_a, kept_b, sends_b, dwin = tie(buf_a, kept_b, sends_b, dwin)
        gots_a = spread(buf_a, *wide)
        gots_b = swap(sends_b, near[1])

        dm0, grads_c, small_c, bias_c = run_heads(0, qkv, prob, dwin, h1, put, hm)
        buf_a, gots_a, kept_b, gots_b, dm0, dwin = tie(buf_a, gots_a, kept_b, gots_b, dm0, dwin)
        buf_a = inner_back(back(buf_a, gots_a, *wide))
        kept_b, sends_b = split_sends(inner(added(kept_b, *gots_b)), *wide)
        buf_a, kept_b, sends_b, dwin = tie(buf_a, kept_b, sends_b, dwin)
        gots_a = spread(buf_a, *near)
        gots_b = swap(sends_b, wide[1])

        dm1, grads_d, small_d, bias_d = run_heads(1, qkv, prob, dwin, h1, put, hm)
        send, keep = core_halves([grads_c, gp, grads_d])
        kept_b, gots_b, send, keep, dm1 = tie(kept_b, gots_b, send, keep, dm1)
        got = across(send)
        buf_b = added(kept_b, *gots_b)
        kept, sends = split_sends(added(keep, got), *near)
        buf_b, kept, sends, dm1 = tie(buf_b, kept, sends, dm1)
        gots = swap(sends, near[1])
        gots_b = spread(buf_b, *wide)

        grad_images, small_end = run_final(images, dmid, dm0, dm1, qkvw, vec)
        kept, gots, buf_a, gots_a, buf_b, gots_b, bias_c, bias_d, small_end = tie(
            kept, gots, buf_a, gots_a, buf_b, gots_b, bias_c, bias_d, small_end
        )
        bias_sum = jnp.concatenate([bias_c, bias_d], axis=0)
        by_head = bias_sum.reshape(GROUPS, KEEP, PACK, WPAD).transpose(0, 2, 1, 3)
        table_grad = lax.dot_general(
            by_head.reshape(HEADS, -1), onehot.astype(f32), (((1,), (1,)), ((), ())),
            precision=HIGH, preferred_element_type=f32,
        )
        table_rows = jnp.pad(table_grad, ((0, 0), (0, half - TABLE)))
        fbias = [fbias_a[0], fbias_b[0], fbias_a[1], fbias_b[1]]
        rows = jnp.concatenate([small_end[0:2], small_mid[0:3], cotsum, *fbias], axis=0)
        small = jnp.concatenate(
            [rows[:, :half], rows[:, half:], small_c[0:2], small_d[0:2], table_rows], axis=0
        )

        buf = added(kept, *gots)
        for base, stride in digits[1:]:
            kept, sends = split_sends(buf, base, stride)
            extra = two_parts(small)
            cut = kept.shape[0]
            gots = swap([jnp.concatenate([value, extra], axis=0) for value in sends], stride)
            buf = added(kept, *[value[:cut] for value in gots])
            for value in gots:
                small = small + one_part(value[cut:])

        buf_a = back(buf_a, gots_a, *near)
        buf_b = inner_back(back(buf_b, gots_b, *wide))
        buf_b = back(buf_b, spread(buf_b, *near), *near)
        for base, stride in reversed(digits[1:]):
            buf = back(buf, swap([buf] * (base - 1), stride), base, stride)
        base, stride = digits[0]
        cut = buf.shape[0]
        extra = two_parts(small)
        gots = swap([jnp.concatenate([buf, extra], axis=0)] * (base - 1), stride)
        buf = back(buf, [value[:cut] for value in gots], base, stride)
        for value in gots:
            small = small + one_part(value[cut:])
        small = small + across(small)
        sum_a, sum_b, sum_c = buf_a.astype(f32), buf_b.astype(f32), buf.astype(f32)

        n = 2 + 3 + 1 + 4
        mine = lax.dynamic_slice(small, (shard * n, 0), (n, half))
        sides = small[2 * n : 2 * n + 4]
        query_sum, value_sum = [
            lax.dynamic_index_in_dim(sides[i::2], shard, 0, keepdims=False) for i in range(2)
        ]
        own_table = lax.dynamic_slice(
            small, (2 * n + 4 + shard * (HEADS // 2), 0), (HEADS // 2, half)
        )[:, :TABLE].T
        fsum = small[: 2 * n].reshape(2, n, half)[:, 6:]
        own_fb = lax.dynamic_slice(fsum, (0, 2 * shard, 0), (2, 2, half))
        own_fb = own_fb.transpose(1, 0, 2).reshape(-1)
        grad_fc2 = jnp.concatenate([sum_a[:BLOCK], sum_b[:BLOCK]], axis=0)
        grad_fc1 = jnp.concatenate(
            [sum_a[BLOCK : BLOCK + half], sum_b[BLOCK : BLOCK + half],
             sum_a[BLOCK + half :], sum_b[BLOCK + half :]], axis=1,
        )
        start = 3 * half + D
        grad_qkv = jnp.concatenate(
            [sum_c[at + b * half : at + (b + 1) * half] for b in range(3) for at in (0, start)],
            axis=1,
        )
        grad_proj = jnp.concatenate(
            [sum_c[3 * half : 4 * half], sum_c[4 * half : 5 * half]], axis=1
        )
        return (
            output.transpose(2, 0, 1, 3), grad_images.transpose(2, 0, 1, 3),
            mine[0], mine[1], grad_qkv, query_sum, value_sum, own_table,
            grad_proj, mine[4], mine[2], mine[3], grad_fc1, own_fb, grad_fc2, mine[5],
        )

    return shards


def solution(mesh):
    return jax.shard_map(
        make_shards(mesh.shape["replica"]),
        mesh=mesh,
        in_specs=(
            P(("replica", "shard"), None, None, None),
            P(("replica", "shard"), None, None, None),
            P(("replica", "shard")),
            P(),
            P(),
            P("shard"),
            P("shard"),
            P("shard", None),
            P("shard"),
            P("shard"),
            P(None, "shard"),
            P("shard", None),
            P("shard"),
            P("shard"),
            P("shard"),
            P("shard", None),
            P("shard"),
            P("shard", None),
            P("shard"),
        ),
        out_specs=(
            P(("replica", "shard"), None, None, None),
            P(("replica", "shard"), None, None, None),
            P("shard"),
            P("shard"),
            P("shard", None),
            P("shard"),
            P("shard"),
            P(None, "shard"),
            P("shard", None),
            P("shard"),
            P("shard"),
            P("shard"),
            P("shard", None),
            P("shard"),
            P("shard", None),
            P("shard"),
        ),
        check_vma=False,
    )
```

```python
import functools

import jax
import jax.numpy as jnp
import numpy as np
from jax import lax
from jax.experimental import pallas as pl
from jax.experimental.pallas import tpu as pltpu
from jax.sharding import PartitionSpec as P

D = 512
HEADS = 16
HEAD = 32
FF = 2048
SIDE = 14
WIN = 7
SHIFT = 3
TABLE = 169
EPSILON = 1e-05
MASK_FILL = -100.0
PAD_FILL = -1e30
SCALE = HEAD**-0.5
HIGH = lax.Precision.HIGHEST

TOKENS = WIN * WIN
CELLS = SIDE // WIN
WINDOWS = CELLS**2
IMGS = 8
WPAD = 64
WROWS = IMGS * WPAD
DROWS = TOKENS * IMGS
PACK = 4
GROUPS = HEADS // PACK
GCOLS = PACK * HEAD
LANES = PACK * WPAD
SPLIT = 2
PART = GROUPS // SPLIT
PCOLS = PART * GCOLS
BLOCK = 512
BATCH = 16
KEEP = 56

f32 = jnp.float32
bf16 = jnp.bfloat16


def window_places():
    take = np.zeros((WROWS, DROWS), np.float32)
    for i in range(IMGS):
        for t in range(TOKENS):
            take[i * WPAD + t, t * IMGS + i] = 1
    return take


def dot(a, b):
    return lax.dot_general(a, b, (((1,), (0,)), ((), ())), preferred_element_type=f32)


def dot_nt(a, b):
    return lax.dot_general(a, b, (((1,), (1,)), ((), ())), preferred_element_type=f32)


def dot_tn(a, b):
    return lax.dot_general(a, b, (((0,), (0,)), ((), ())), preferred_element_type=f32)


def normed(x):
    centred = x - jnp.mean(x, axis=-1, keepdims=True)
    rstd = lax.rsqrt(jnp.mean(centred * centred, axis=-1, keepdims=True) + EPSILON)
    return centred * rstd, rstd


def norm_back(grad, gain, hat, rstd):
    g = grad * gain
    mean_g = jnp.mean(g, axis=-1, keepdims=True)
    mean_gh = jnp.mean(g * hat, axis=-1, keepdims=True)
    return rstd * (g - mean_g - hat * mean_gh)


def spread_heads(block, head_mask):
    return jnp.concatenate([block] * PACK, axis=0) * head_mask


def gather_heads(result):
    lane = lax.broadcasted_iota(jnp.int32, (WPAD, GCOLS), 1) // HEAD
    parts = [result[h * WPAD : (h + 1) * WPAD] for h in range(PACK)]
    out = parts[PACK - 1]
    for h in range(PACK - 2, -1, -1):
        out = jnp.where(lane == h, parts[h], out)
    return out


def token_places(place):
    row0 = (place // CELLS) * WIN + SHIFT
    col0 = (place % CELLS) * WIN + SHIFT
    for i in range(WIN):
        r = row0 + i
        r = jnp.where(r >= SIDE, r - SIDE, r)
        for j in range(WIN):
            c = col0 + j
            yield (i * WIN + j) * IMGS, r, jnp.where(c >= SIDE, c - SIDE, c)


def load_window(rows, ref, place):
    for at, r, c in token_places(place):
        rows[at : at + IMGS] = ref[r, c].astype(f32)
    return rows[...]


def store_window(ref, value, place):
    for at, r, c in token_places(place):
        ref[r, c] = value[at : at + IMGS].astype(bf16)


def join_rows(full, own_ref, other_ref):
    half = full.shape[0] // 2
    first = lax.axis_index("shard") == 0

    @pl.when(first)
    def _():
        full[0:half] = own_ref[...]
        full[half:] = other_ref[...]

    @pl.when(jnp.logical_not(first))
    def _():
        full[0:half] = other_ref[...]
        full[half:] = own_ref[...]


def join_vectors(vec, own_ref, other_ref):
    first = lax.axis_index("shard") == 0
    own, other = own_ref[...].astype(f32), other_ref[...].astype(f32)
    vec[:, 0 : D // 2] = jnp.where(first, own, other)
    vec[:, D // 2 :] = jnp.where(first, other, own)


G1, B1, QB, VB, PB, G2, B2, F2B, FB = range(9)
VROWS = 12


def forward_kernel(
    count_ref, img_ref, og_ref, take_ref, put_ref, qw0_ref, qw1_ref, pw0_ref, pw1_ref,
    vec0_ref, vec1_ref, pos_ref, mask_ref, hm_ref,
    qkv_out, prob_out, h1_out, att_out, mid_out, h2_out, cot_out, cotsum_out,
    rows_in, att, qkvw_ref, pw_ref, vec,
):
    place = pl.program_id(0)

    @pl.when(place == 0)
    def _():
        cotsum_out[...] = jnp.zeros_like(cotsum_out)
        join_rows(qkvw_ref, qw0_ref, qw1_ref)
        join_rows(pw_ref, pw0_ref, pw1_ref)
        join_vectors(vec, vec0_ref, vec1_ref)

    def row(at):
        return vec[at : at + 1]

    image = lax.broadcasted_iota(jnp.int32, (DROWS, D), 0) % IMGS
    cot = jnp.where(image < count_ref[0], load_window(rows_in, og_ref, place), 0.0)
    cot_out[...] = cot.astype(bf16)
    cotsum_out[...] += jnp.sum(cot, axis=0, keepdims=True)

    x = load_window(rows_in, img_ref, place)
    hat, _ = normed(x)
    h1 = (hat * row(G1) + row(B1)).astype(bf16)
    h1_out[...] = h1
    tiles = dot(take_ref[...], h1).astype(bf16)
    qkv_out[:, 0:D] = (dot(tiles, qkvw_ref[:, 0:D]) + row(QB)).astype(bf16)
    qkv_out[:, D : 2 * D] = dot(tiles, qkvw_ref[:, D : 2 * D]).astype(bf16)
    qkv_out[:, 2 * D : 3 * D] = (dot(tiles, qkvw_ref[:, 2 * D : 3 * D]) + row(VB)).astype(bf16)
    head_mask = hm_ref[...]
    units = [(i, g) for g in range(GROUPS) for i in range(IMGS)]
    for at in range(0, len(units), BATCH):
        batch = units[at : at + BATCH]
        rows = [slice(i * WPAD, (i + 1) * WPAD) for i, _ in batch]
        cols = [slice(g * GCOLS, (g + 1) * GCOLS) for _, g in batch]
        wide = [spread_heads(qkv_out[r, c], head_mask) for r, c in zip(rows, cols)]
        keys = [qkv_out[r, D + c.start : D + c.stop] for r, c in zip(rows, cols)]
        s = [dot_nt(k, q)[:KEEP] for k, q in zip(keys, wide)]
        s = [v * SCALE + pos_ref[g] + mask_ref[...] for v, (_, g) in zip(s, batch)]
        e = [jnp.exp(v - jnp.max(v, axis=0, keepdims=True)) for v in s]
        p = [v / jnp.sum(v, axis=0, keepdims=True) for v in e]
        zero = jnp.zeros((WPAD - KEEP, LANES), f32)
        p = [jnp.concatenate([v, zero], axis=0).astype(bf16) for v in p]
        for v, (i, g) in zip(p, batch):
            prob_out[g, i] = v
        values = [qkv_out[r, 2 * D + c.start : 2 * D + c.stop] for r, c in zip(rows, cols)]
        found = [dot_tn(v, w) for v, w in zip(p, values)]
        for r, c, v in zip(rows, cols, found):
            att[r, c] = gather_heads(v).astype(bf16)
    a = dot(put_ref[...], att[...]).astype(bf16)
    att_out[...] = a
    middle = x + (dot(a, pw_ref[...]) + row(PB))
    mid_out[...] = middle
    hat2, _ = normed(middle)
    h2_out[...] = (hat2 * row(G2) + row(B2)).astype(bf16)


def ffn_kernel(which, last, *refs):
    refs = list(refs)
    h2_ref, cot_ref, f10_ref, f11_ref, f20_ref, f21_ref, vec0_ref, vec1_ref = refs[:8]
    refs = refs[8:]
    if last:
        oin_ref, din_ref, mid_ref = refs[:3]
        refs = refs[3:]
    send, keep, bias_out, out_ref, dh2_ref = refs[:5]
    acc1, acc2, oacc, dacc, f1_ref, f2_ref, vec, fbias = refs[5:]
    j, c = pl.program_id(0), pl.program_id(1)

    @pl.when(c == 0)
    def _():
        mine = lax.axis_index("shard") == j
        join_rows(f1_ref, f10_ref, f11_ref)
        join_vectors(vec, vec0_ref, vec1_ref)

        def owner_parts(f2, vectors):
            f2_ref[...] = f2[...]
            for b in range(BLOCK // (D // 2)):
                at = FB + which * (BLOCK // (D // 2)) + b
                fbias[:, b * D // 2 : (b + 1) * D // 2] = vectors[at : at + 1].astype(f32)

        @pl.when(mine)
        def _():
            owner_parts(f20_ref, vec0_ref)

        @pl.when(jnp.logical_not(mine))
        def _():
            owner_parts(f21_ref, vec1_ref)

    h2 = h2_ref[...]
    cot = cot_ref[...]
    hidden = dot(h2, f1_ref[...]) + fbias[...]
    dact = dot_nt(cot, f2_ref[...])
    bell = jnp.exp(hidden * hidden * -0.5)
    base = 1.0 + jnp.abs(hidden) * (0.3275911 * 0.5**0.5)
    t = pl.reciprocal(base, approx=True)
    t = t * (2.0 - base * t)
    half = t * (
        0.127414796
        + t * (-0.142248368 + t * (0.7107068705 + t * (-0.7265760135 + t * 0.5307027145)))
    )
    half = half * bell
    phi = jnp.where(hidden > 0, 1.0 - half, half)
    act = (hidden * phi).astype(bf16)
    dhid = dact * (phi + hidden * bell * 0.3989422804014327)
    dhid_low = dhid.astype(bf16)

    g2 = dot_tn(act, cot)
    g1 = dot_tn(h2, dhid_low)
    fb = jnp.sum(dhid, axis=0, keepdims=True)
    o = dot(act, f2_ref[...])
    d = dot_nt(dhid_low, f1_ref[...])

    acc1[...] = jnp.where(c == 0, 0.0, acc1[...]) + g1
    acc2[...] = jnp.where(c == 0, 0.0, acc2[...]) + g2
    bias_out[0] = jnp.where(c == 0, 0.0, bias_out[0]) + fb
    o = jnp.where(j == 0, 0.0, oacc[c]) + o
    d = jnp.where(j == 0, 0.0, dacc[c]) + d
    oacc[c] = o
    dacc[c] = d
    if last:
        dh2_ref[...] = d + din_ref[...]
        store_window(out_ref, mid_ref[...] + (o + oin_ref[...]) + vec[F2B : F2B + 1], c)
    else:
        dh2_ref[...] = d
        out_ref[...] = o

    half_rows = D // 2

    @pl.when(c == pl.num_programs(1) - 1)
    def _():
        mine = lax.axis_index("shard")

        def hand_out(owner, at, value):
            @pl.when(owner == mine)
            def _():
                keep[at] = value

            @pl.when(owner != mine)
            def _():
                send[at] = value

        hand_out(j, slice(0, BLOCK), acc2[...].astype(bf16))
        place = pl.ds(pl.multiple_of(BLOCK + j * half_rows, half_rows), half_rows)
        hand_out(0, place, acc1[0:half_rows].astype(bf16))
        hand_out(1, place, acc1[half_rows:D].astype(bf16))


def middle_kernel(
    cot_ref, dh2_ref, mid_ref, att_ref, take_ref, pw0_ref, pw1_ref, vec0_ref, vec1_ref,
    dmid_out, dwin_out, grads, small, gp, pw_ref, vec,
):
    place = pl.program_id(0)

    @pl.when(place == 0)
    def _():
        small[...] = jnp.zeros_like(small)
        gp[...] = jnp.zeros_like(gp)
        join_rows(pw_ref, pw0_ref, pw1_ref)
        join_vectors(vec, vec0_ref, vec1_ref)

    hat2, rstd2 = normed(mid_ref[...])
    dh2 = dh2_ref[...]
    small[0:1] += jnp.sum(dh2 * hat2, axis=0, keepdims=True)
    small[1:2] += jnp.sum(dh2, axis=0, keepdims=True)
    dmid = cot_ref[...].astype(f32) + norm_back(dh2, vec[G2 : G2 + 1], hat2, rstd2)
    small[2:3] += jnp.sum(dmid, axis=0, keepdims=True)
    dmid_out[...] = dmid
    dbr = dmid.astype(bf16)
    gp[...] += dot_tn(att_ref[...], dbr)
    datt = dot_nt(dbr, pw_ref[...]).astype(bf16)
    dwin_out[...] = dot(take_ref[...], datt).astype(bf16)

    @pl.when(place == pl.num_programs(0) - 1)
    def _():
        half = D // 2
        for o in range(2):
            for b in range(2):
                grads[o, b * half : (b + 1) * half] = gp[
                    o * half : (o + 1) * half, b * half : (b + 1) * half
                ].astype(bf16)


def heads_kernel(
    q_ref, k_ref, v_ref, prob_ref, dwin_ref, h1_ref, put_ref, hm_ref,
    dm_out, grads, small, bias_out, dmix, gq,
):
    place = pl.program_id(0)

    @pl.when(place == 0)
    def _():
        small[...] = jnp.zeros_like(small)
        bias_out[...] = jnp.zeros_like(bias_out)
        gq[...] = jnp.zeros_like(gq)

    head_mask = hm_ref[...]
    units = [(i, g) for g in range(PART) for i in range(IMGS)]
    zero = jnp.zeros((WPAD - KEEP, LANES), f32)
    for at in range(0, len(units), BATCH):
        batch = units[at : at + BATCH]
        rows = [slice(i * WPAD, (i + 1) * WPAD) for i, _ in batch]
        cols = [slice(g * GCOLS, (g + 1) * GCOLS) for _, g in batch]
        wide = [spread_heads(dwin_ref[r, c], head_mask) for r, c in zip(rows, cols)]
        dp = [dot_nt(v_ref[r, c], da)[:KEEP] for r, c, da in zip(rows, cols, wide)]
        low = [prob_ref[g, i] for i, g in batch]
        dv = [dot(p, da) for p, da in zip(low, wide)]
        p = [v.astype(f32)[:KEEP] for v in low]
        inner = [jnp.sum(x * y, axis=0, keepdims=True) for x, y in zip(dp, p)]
        ds = [(y * (x - n)).astype(bf16).astype(f32) for x, y, n in zip(dp, p, inner)]
        for v, (_, g) in zip(ds, batch):
            bias_out[g] += v
        ds = [jnp.concatenate([v, zero], axis=0).astype(bf16) for v in ds]
        dq = [dot_tn(v, k_ref[r, c]) for v, r, c in zip(ds, rows, cols)]
        queries = [spread_heads(q_ref[r, c], head_mask) for r, c in zip(rows, cols)]
        dk = [dot(v, q) for v, q in zip(ds, queries)]
        for r, c, x, y, w in zip(rows, cols, dq, dk, dv):
            dmix[r, c] = (gather_heads(x) * SCALE).astype(bf16)
            dmix[r, PCOLS + c.start : PCOLS + c.stop] = (y * SCALE).astype(bf16)
            dmix[r, 2 * PCOLS + c.start : 2 * PCOLS + c.stop] = w.astype(bf16)
    small[0:1] += jnp.sum(dmix[:, 0:PCOLS].astype(f32), axis=0, keepdims=True)
    small[1:2] += jnp.sum(dmix[:, 2 * PCOLS : 3 * PCOLS].astype(f32), axis=0, keepdims=True)
    dm = dot(put_ref[...], dmix[...]).astype(bf16)
    dm_out[...] = dm
    gq[...] += dot_tn(h1_ref[...], dm)

    @pl.when(place == pl.num_programs(0) - 1)
    def _():
        half = D // 2
        for o in range(2):
            for b in range(3):
                grads[o, b * half : (b + 1) * half] = gq[
                    o * half : (o + 1) * half, b * PCOLS : (b + 1) * PCOLS
                ].astype(bf16)


def final_kernel(
    img_ref, dmid_ref, dm0_ref, dm1_ref, qw0_ref, qw1_ref, vec0_ref, vec1_ref,
    out_ref, small, rows_in, qkvw_ref, vec,
):
    place = pl.program_id(0)

    @pl.when(place == 0)
    def _():
        small[...] = jnp.zeros_like(small)
        join_rows(qkvw_ref, qw0_ref, qw1_ref)
        join_vectors(vec, vec0_ref, vec1_ref)

    dh1 = None
    for part, ref in enumerate((dm0_ref, dm1_ref)):
        for b in range(3):
            at = b * D + part * PCOLS
            term = dot_nt(ref[:, b * PCOLS : (b + 1) * PCOLS], qkvw_ref[:, at : at + PCOLS])
            dh1 = term if dh1 is None else dh1 + term
    hat1, rstd1 = normed(load_window(rows_in, img_ref, place))
    small[0:1] += jnp.sum(dh1 * hat1, axis=0, keepdims=True)
    small[1:2] += jnp.sum(dh1, axis=0, keepdims=True)
    store_window(out_ref, dmid_ref[...] + norm_back(dh1, vec[G1 : G1 + 1], hat1, rstd1), place)


def far(value):
    return pltpu.with_memory_space_constraint(value, pltpu.HBM)


def all_far(values):
    return [far(value) for value in values]


def whole(shape):
    return pl.BlockSpec(shape, lambda *_: (0,) * len(shape))


def by_place(*dims):
    return pl.BlockSpec((None,) + dims, lambda i: (i,) + (0,) * len(dims))


def params(axes, flops, size):
    return dict(
        compiler_params=pltpu.CompilerParams(
            dimension_semantics=("arbitrary",) * axes, vmem_limit_bytes=24 * 1024 * 1024
        ),
        cost_estimate=pl.CostEstimate(flops=int(flops), bytes_accessed=int(size), transcendentals=0),
    )


IMAGE = (SIDE, SIDE, IMGS, D)


def dense(kind, cols=D):
    return jax.ShapeDtypeStruct((WINDOWS, DROWS, cols), kind)


VECTORS = pltpu.VMEM((VROWS, D), f32)


def run_forward(images, out_grad, count, take, put, qkvw, pw, vec, pos, mask, hm):
    drow = by_place(DROWS, D)
    pair = [whole(qkvw[0].shape)] * 2 + [whole(pw[0].shape)] * 2 + [whole(vec[0].shape)] * 2
    return pl.pallas_call(
        forward_kernel,
        grid=(WINDOWS,),
        in_specs=[
            pl.BlockSpec(memory_space=pltpu.SMEM), whole(IMAGE), whole(IMAGE),
            whole(take.shape), whole(put.shape), *pair,
            whole(pos.shape), by_place(KEEP, LANES), whole(hm.shape),
        ],
        out_specs=[
            by_place(WROWS, 3 * D), by_place(GROUPS, IMGS, WPAD, LANES),
            drow, drow, drow, drow, drow, whole((1, D)),
        ],
        out_shape=[
            pltpu.HBM((WINDOWS, WROWS, 3 * D), bf16),
            pltpu.HBM((WINDOWS, GROUPS, IMGS, WPAD, LANES), bf16),
            pltpu.HBM((WINDOWS, DROWS, D), bf16), pltpu.HBM((WINDOWS, DROWS, D), bf16),
            pltpu.HBM((WINDOWS, DROWS, D), f32), dense(bf16), dense(bf16),
            jax.ShapeDtypeStruct((1, D), f32),
        ],
        scratch_shapes=[
            pltpu.VMEM((DROWS, D), f32), pltpu.VMEM((WROWS, D), bf16),
            pltpu.VMEM((D, 3 * D), bf16), pltpu.VMEM((D, D), bf16), VECTORS,
        ],
        name="forward_attention",
        **params(1, 9e9, 25e6),
    )(count, *all_far([images, out_grad, take, put, *qkvw, *pw, *vec, pos, mask, hm]))


def run_ffn(which, h2, cot, fc1, fc2, vec, finish=None):
    last = finish is not None
    chunk = pl.BlockSpec((None, DROWS, D), lambda j, c: (c, 0, 0))
    late = pl.BlockSpec((None, DROWS, D), lambda j, c: (c * j, 0, 0))
    f1 = pl.BlockSpec((D // 2, BLOCK), lambda j, c: (0, 2 * j + which))
    f2 = pl.BlockSpec((BLOCK, D), lambda j, c: (which, 0))
    vecs = whole(vec[0].shape)
    in_specs = [chunk, chunk, f1, f1, f2, f2, vecs, vecs]
    args = [h2, cot, *all_far([*fc1, *fc2, *vec])]
    out, out_spec = pltpu.HBM((WINDOWS, DROWS, D), f32), late
    if last:
        in_specs += [late, late, late]
        args += all_far(finish)
        out, out_spec = jax.ShapeDtypeStruct(IMAGE, bf16), whole(IMAGE)
    return pl.pallas_call(
        functools.partial(ffn_kernel, which, last),
        grid=(2, WINDOWS),
        in_specs=in_specs,
        out_specs=[
            *[whole((2 * BLOCK, D))] * 2, pl.BlockSpec((1, 1, BLOCK), lambda j, c: (j, 0, 0)),
            out_spec, late,
        ],
        out_shape=[
            *[jax.ShapeDtypeStruct((2 * BLOCK, D), bf16)] * 2,
            jax.ShapeDtypeStruct((2, 1, BLOCK), f32), out,
            pltpu.HBM((WINDOWS, DROWS, D), f32),
        ],
        scratch_shapes=[
            pltpu.VMEM((D, BLOCK), f32), pltpu.VMEM((BLOCK, D), f32),
            pltpu.VMEM((WINDOWS, DROWS, D), f32), pltpu.VMEM((WINDOWS, DROWS, D), f32),
            pltpu.VMEM((D, BLOCK), bf16), pltpu.VMEM((BLOCK, D), bf16), VECTORS,
            pltpu.VMEM((1, BLOCK), f32),
        ],
        name="ffn",
        **params(2, 2 * 12 * WINDOWS * DROWS * D * BLOCK, 20e6),
    )(*args)


def run_middle(cot, dh2, mid, att, take, pw, vec):
    drow = by_place(DROWS, D)
    return pl.pallas_call(
        middle_kernel,
        grid=(WINDOWS,),
        in_specs=[
            drow, drow, drow, drow, whole(take.shape), *[whole(pw[0].shape)] * 2,
            *[whole(vec[0].shape)] * 2,
        ],
        out_specs=[drow, by_place(WROWS, D), whole((2, D, D // 2)), whole((8, D))],
        out_shape=[
            dense(f32), jax.ShapeDtypeStruct((WINDOWS, WROWS, D), bf16),
            jax.ShapeDtypeStruct((2, D, D // 2), bf16), jax.ShapeDtypeStruct((8, D), f32),
        ],
        scratch_shapes=[pltpu.VMEM((D, D), f32), pltpu.VMEM((D, D), bf16), VECTORS],
        name="middle_backward",
        **params(1, 3e9, 10e6),
    )(*all_far([cot, dh2, mid, att, take, *pw, *vec]))


def run_heads(part, qkv, prob, dwin, h1, put, hm):
    def columns(at):
        return pl.BlockSpec((None, WROWS, PCOLS), lambda i: (i, 0, at))

    rows = 3 * (D // 2)
    return pl.pallas_call(
        heads_kernel,
        grid=(WINDOWS,),
        in_specs=[
            columns(part), columns(SPLIT + part), columns(2 * SPLIT + part),
            pl.BlockSpec((None, PART, IMGS, WPAD, LANES), lambda i: (i, part, 0, 0, 0)),
            columns(part), by_place(DROWS, D), whole(put.shape), whole(hm.shape),
        ],
        out_specs=[
            by_place(DROWS, 3 * PCOLS), whole((2, rows, D // 2)), whole((8, PCOLS)),
            whole((PART, KEEP, LANES)),
        ],
        out_shape=[
            pltpu.HBM((WINDOWS, DROWS, 3 * PCOLS), bf16),
            jax.ShapeDtypeStruct((2, rows, D // 2), bf16),
            jax.ShapeDtypeStruct((8, PCOLS), f32),
            jax.ShapeDtypeStruct((PART, KEEP, LANES), f32),
        ],
        scratch_shapes=[
            pltpu.VMEM((WROWS, 3 * PCOLS), bf16), pltpu.VMEM((D, 3 * PCOLS), f32),
        ],
        name="attention_backward",
        **params(1, 4e9, 10e6),
    )(*all_far([qkv, qkv, qkv, prob]), dwin, *all_far([h1, put, hm]))


def run_final(images, dmid, dm0, dm1, qkvw, vec):
    return pl.pallas_call(
        final_kernel,
        grid=(WINDOWS,),
        in_specs=[
            whole(IMAGE), by_place(DROWS, D), by_place(DROWS, 3 * PCOLS),
            by_place(DROWS, 3 * PCOLS), *[whole(qkvw[0].shape)] * 2, *[whole(vec[0].shape)] * 2,
        ],
        out_specs=[whole(IMAGE), whole((8, D))],
        out_shape=[jax.ShapeDtypeStruct(IMAGE, bf16), jax.ShapeDtypeStruct((8, D), f32)],
        scratch_shapes=[pltpu.VMEM((DROWS, D), f32), pltpu.VMEM((D, 3 * D), bf16), VECTORS],
        name="final_backward",
        **params(1, 3e9, 10e6),
    )(far(images), dmid, *all_far([dm0, dm1, *qkvw, *vec]))


def digits_of(n):
    digits, stride = [], 1
    while n > 1:
        base = 4 if n % 4 == 0 else 2
        digits.append((base, stride))
        stride *= base
        n //= base
    return digits


def make_shards(replicas):
    axes = ("replica", "shard")
    core_pairs = [(r * 2 + s, r * 2 + 1 - s) for r in range(replicas) for s in range(2)]
    digits = digits_of(replicas)

    def across(value):
        return lax.ppermute(value, axes, core_pairs)

    def partner(value, k, stride):
        pairs = [(r * 2 + s, (r ^ (k * stride)) * 2 + s) for r in range(replicas) for s in range(2)]
        return lax.ppermute(value, axes, pairs)

    def place(base, stride):
        return (lax.axis_index("replica") // stride) % base

    def pick(value, index):
        return lax.dynamic_index_in_dim(value, index, 0, keepdims=False)

    def in_order(parts, mine):
        base = len(parts)
        laid = []
        for at in range(base):
            value = parts[at]
            for c in range(1, base):
                value = jnp.where(mine == c, parts[at ^ c], value)
            laid.append(value)
        return jnp.stack(laid)

    def both_halves(value):
        other = across(value)
        first = lax.axis_index("shard") == 0
        return jnp.where(first, value, other), jnp.where(first, other, value)

    def tie(*values):
        return lax.optimization_barrier(values)

    def core_halves(parts):
        s = lax.axis_index("shard")
        return [
            jnp.concatenate([pick(part, at) for part in parts], axis=0) for at in (1 - s, s)
        ]

    def added(*values):
        total = values[0].astype(f32)
        for value in values[1:]:
            total = total + value.astype(f32)
        return total.astype(bf16)

    def split_sends(buf, base, stride):
        mine = place(base, stride)
        view = buf.reshape(base, buf.shape[0] // base, buf.shape[1])
        return pick(view, mine), [pick(view, mine ^ k) for k in range(1, base)]

    def swap(sends, stride):
        return [partner(value, k + 1, stride) for k, value in enumerate(sends)]

    def two_parts(value):
        top = lax.reduce_precision(value, 8, 7)
        return jnp.concatenate([top.astype(bf16), (value - top).astype(bf16)], axis=0)

    def one_part(rows):
        half = rows.shape[0] // 2
        return rows[:half].astype(f32) + rows[half:].astype(f32)

    def shards(
        images, out_grad, image_counts, regions, relative_index,
        norm1_gain, norm1_bias, qkv_weight, query_bias, value_bias, bias_table,
        proj_weight, proj_bias, norm2_gain, norm2_bias, fc1_weight, fc1_bias, fc2_weight, fc2_bias,
    ):
        shard = lax.axis_index("shard")
        half = D // 2
        images = images.transpose(1, 2, 0, 3)
        out_grad = out_grad.transpose(1, 2, 0, 3)
        qkvw = (qkv_weight, across(qkv_weight))
        vectors = [
            norm1_gain, norm1_bias, query_bias, value_bias,
            proj_bias, norm2_gain, norm2_bias, fc2_bias,
        ] + [fc1_bias[i * half : (i + 1) * half] for i in range(VROWS - FB)]
        at_row = lax.broadcasted_iota(jnp.int32, (VROWS, half), 0)
        packed = jnp.zeros((VROWS, half), bf16)
        for i, value in enumerate(vectors):
            packed = jnp.where(at_row == i, value[None, :], packed)
        vec = (packed, across(packed))
        table = jnp.concatenate(both_halves(bias_table.T), axis=0)
        pw = (proj_weight, across(proj_weight))
        fc1 = (fc1_weight, across(fc1_weight))
        fc2 = (fc2_weight, across(fc2_weight))

        index = jnp.pad(
            relative_index.T, ((0, KEEP - TOKENS), (0, WPAD - TOKENS)), constant_values=-1
        )
        onehot = (
            index.reshape(1, -1) == jnp.arange(TABLE, dtype=jnp.int32)[:, None]
        ).astype(bf16)
        pos = dot(table, onehot).reshape(GROUPS, PACK, KEEP, WPAD)
        pos = pos.transpose(0, 2, 1, 3).reshape(GROUPS, KEEP, LANES)
        labels = regions.reshape(CELLS, WIN, CELLS, WIN).transpose(0, 2, 1, 3)
        labels = labels.reshape(WINDOWS, TOKENS)
        differ = labels[:, :, None] != labels[:, None, :]
        mask = jnp.where(differ, MASK_FILL, 0.0).astype(f32)
        mask = jnp.pad(mask, ((0, 0), (0, 0), (0, WPAD - TOKENS)))
        mask = jnp.pad(mask, ((0, 0), (0, KEEP - TOKENS), (0, 0)), constant_values=PAD_FILL)
        mask = jnp.tile(mask, (1, 1, PACK))

        take_np = window_places()
        take = jnp.asarray(take_np, bf16)
        put = jnp.asarray(take_np.T, bf16)
        hm = jnp.asarray(
            (np.arange(LANES)[:, None] // WPAD) == (np.arange(GCOLS)[None, :] // HEAD), bf16
        )

        qkv, prob, h1, att, mid, h2, cot, cotsum = run_forward(
            images, out_grad, image_counts, take, put, qkvw, pw, vec, pos, mask, hm
        )
        near, wide = digits[0], digits[-1]

        def inner(buf):
            for base, stride in digits[1:-1]:
                kept, sends = split_sends(buf, base, stride)
                buf = added(kept, *swap(sends, stride))
            return buf

        def back(buf, gots, base, stride):
            return in_order([buf] + gots, place(base, stride)).reshape(-1, buf.shape[1])

        def inner_back(buf):
            for base, stride in reversed(digits[1:-1]):
                buf = back(buf, swap([buf] * (base - 1), stride), base, stride)
            return buf

        def spread(buf, base, stride):
            return swap([buf] * (base - 1), stride)

        send, keep, fbias_a, oacc, dacc = run_ffn(0, h2, cot, fc1, fc2, vec)
        kept_a, sends_a = split_sends(added(keep, across(send)), *near)
        kept_a, sends_a, h2 = tie(kept_a, sends_a, h2)
        gots_a = swap(sends_a, near[1])

        send, keep, fbias_b, output, dh2 = run_ffn(
            1, h2, cot, fc1, fc2, vec, (oacc, dacc, mid)
        )
        kept_a, gots_a, send, dh2 = tie(kept_a, gots_a, send, dh2)
        got = across(send)
        kept_a, sends_a = split_sends(inner(added(kept_a, *gots_a)), *wide)
        kept_a, sends_a, dh2 = tie(kept_a, sends_a, dh2)
        gots_a = swap(sends_a, wide[1])

        dmid, dwin, gp, small_mid = run_middle(cot, dh2, mid, att, take, pw, vec)
        kept_a, gots_a, got, dwin = tie(kept_a, gots_a, got, dwin)
        kept_b, sends_b = split_sends(added(keep, got), *near)
        buf_a = added(kept_a, *gots_a)
        buf_a, kept_b, sends_b, dwin = tie(buf_a, kept_b, sends_b, dwin)
        gots_a = spread(buf_a, *wide)
        gots_b = swap(sends_b, near[1])

        dm0, grads_c, small_c, bias_c = run_heads(0, qkv, prob, dwin, h1, put, hm)
        buf_a, gots_a, kept_b, gots_b, dm0, dwin = tie(buf_a, gots_a, kept_b, gots_b, dm0, dwin)
        buf_a = inner_back(back(buf_a, gots_a, *wide))
        kept_b, sends_b = split_sends(inner(added(kept_b, *gots_b)), *wide)
        buf_a, kept_b, sends_b, dwin = tie(buf_a, kept_b, sends_b, dwin)
        gots_a = spread(buf_a, *near)
        gots_b = swap(sends_b, wide[1])

        dm1, grads_d, small_d, bias_d = run_heads(1, qkv, prob, dwin, h1, put, hm)
        send, keep = core_halves([grads_c, gp, grads_d])
        send, dm1 = tie(send, dm1)
        kept, sends = split_sends(added(keep, across(send)), *near)
        kept, sends, dm1 = tie(kept, sends, dm1)
        gots = swap(sends, near[1])

        grad_images, small_end = run_final(images, dmid, dm0, dm1, qkvw, vec)
        kept, gots, buf_a, gots_a, kept_b, gots_b, bias_c, bias_d, small_end = tie(
            kept, gots, buf_a, gots_a, kept_b, gots_b, bias_c, bias_d, small_end
        )
        bias_sum = jnp.concatenate([bias_c, bias_d], axis=0)
        by_head = bias_sum.reshape(GROUPS, KEEP, PACK, WPAD).transpose(0, 2, 1, 3)
        table_grad = lax.dot_general(
            by_head.reshape(HEADS, -1), onehot.astype(f32), (((1,), (1,)), ((), ())),
            precision=HIGH, preferred_element_type=f32,
        )
        table_rows = jnp.pad(table_grad, ((0, 0), (0, half - TABLE)))
        fbias = [fbias_a[0], fbias_b[0], fbias_a[1], fbias_b[1]]
        rows = jnp.concatenate([small_end[0:2], small_mid[0:3], cotsum, *fbias], axis=0)
        small = jnp.concatenate(
            [rows[:, :half], rows[:, half:], small_c[0:2], small_d[0:2], table_rows], axis=0
        )

        buf = added(kept, *gots)
        for base, stride in digits[1:]:
            kept, sends = split_sends(buf, base, stride)
            extra = two_parts(small)
            cut = kept.shape[0]
            sends = [jnp.concatenate([value, extra], axis=0) for value in sends]
            sends, kept_b, gots_b, buf_a, gots_a = tie(sends, kept_b, gots_b, buf_a, gots_a)
            gots = swap(sends, stride)
            buf = added(kept, *[value[:cut] for value in gots])
            for value in gots:
                small = small + one_part(value[cut:])

        buf_a = back(buf_a, gots_a, *near)
        buf_b = added(kept_b, *gots_b)
        buf_b = inner_back(back(buf_b, spread(buf_b, *wide), *wide))
        buf_b = back(buf_b, spread(buf_b, *near), *near)
        for base, stride in reversed(digits[1:]):
            buf = back(buf, swap([buf] * (base - 1), stride), base, stride)
        base, stride = digits[0]
        cut = buf.shape[0]
        extra = two_parts(small)
        gots = swap([jnp.concatenate([buf, extra], axis=0)] * (base - 1), stride)
        buf = back(buf, [value[:cut] for value in gots], base, stride)
        for value in gots:
            small = small + one_part(value[cut:])
        small = small + across(small)
        sum_a, sum_b, sum_c = buf_a.astype(f32), buf_b.astype(f32), buf.astype(f32)

        n = 2 + 3 + 1 + 4
        mine = lax.dynamic_slice(small, (shard * n, 0), (n, half))
        sides = small[2 * n : 2 * n + 4]
        query_sum, value_sum = [
            lax.dynamic_index_in_dim(sides[i::2], shard, 0, keepdims=False) for i in range(2)
        ]
        own_table = lax.dynamic_slice(
            small, (2 * n + 4 + shard * (HEADS // 2), 0), (HEADS // 2, half)
        )[:, :TABLE].T
        fsum = small[: 2 * n].reshape(2, n, half)[:, 6:]
        own_fb = lax.dynamic_slice(fsum, (0, 2 * shard, 0), (2, 2, half))
        own_fb = own_fb.transpose(1, 0, 2).reshape(-1)
        grad_fc2 = jnp.concatenate([sum_a[:BLOCK], sum_b[:BLOCK]], axis=0)
        grad_fc1 = jnp.concatenate(
            [sum_a[BLOCK : BLOCK + half], sum_b[BLOCK : BLOCK + half],
             sum_a[BLOCK + half :], sum_b[BLOCK + half :]], axis=1,
        )
        start = 3 * half + D
        grad_qkv = jnp.concatenate(
            [sum_c[at + b * half : at + (b + 1) * half] for b in range(3) for at in (0, start)],
            axis=1,
        )
        grad_proj = jnp.concatenate(
            [sum_c[3 * half : 4 * half], sum_c[4 * half : 5 * half]], axis=1
        )
        return (
            output.transpose(2, 0, 1, 3), grad_images.transpose(2, 0, 1, 3),
            mine[0], mine[1], grad_qkv, query_sum, value_sum, own_table,
            grad_proj, mine[4], mine[2], mine[3], grad_fc1, own_fb, grad_fc2, mine[5],
        )

    return shards


def solution(mesh):
    return jax.shard_map(
        make_shards(mesh.shape["replica"]),
        mesh=mesh,
        in_specs=(
            P(("replica", "shard"), None, None, None),
            P(("replica", "shard"), None, None, None),
            P(("replica", "shard")),
            P(),
            P(),
            P("shard"),
            P("shard"),
            P("shard", None),
            P("shard"),
            P("shard"),
            P(None, "shard"),
            P("shard", None),
            P("shard"),
            P("shard"),
            P("shard"),
            P("shard", None),
            P("shard"),
            P("shard", None),
            P("shard"),
        ),
        out_specs=(
            P(("replica", "shard"), None, None, None),
            P(("replica", "shard"), None, None, None),
            P("shard"),
            P("shard"),
            P("shard", None),
            P("shard"),
            P("shard"),
            P(None, "shard"),
            P("shard", None),
            P("shard"),
            P("shard"),
            P("shard"),
            P("shard", None),
            P("shard"),
            P("shard", None),
            P("shard"),
        ),
        check_vma=False,
    )
```

```python
import functools

import jax
import jax.numpy as jnp
import numpy as np
from jax import lax
from jax.experimental import pallas as pl
from jax.experimental.pallas import tpu as pltpu
from jax.sharding import PartitionSpec as P

D = 512
HEADS = 16
HEAD = 32
FF = 2048
SIDE = 14
WIN = 7
SHIFT = 3
TABLE = 169
EPSILON = 1e-05
MASK_FILL = -100.0
PAD_FILL = -1e30
SCALE = HEAD**-0.5
HIGH = lax.Precision.HIGHEST

TOKENS = WIN * WIN
CELLS = SIDE // WIN
WINDOWS = CELLS**2
IMGS = 8
WPAD = 64
WROWS = IMGS * WPAD
DROWS = TOKENS * IMGS
PACK = 4
GROUPS = HEADS // PACK
GCOLS = PACK * HEAD
LANES = PACK * WPAD
SPLIT = 2
PART = GROUPS // SPLIT
PCOLS = PART * GCOLS
BLOCK = 512
BATCH = 16
KEEP = 56

f32 = jnp.float32
bf16 = jnp.bfloat16


def window_places():
    take = np.zeros((WROWS, DROWS), np.float32)
    for i in range(IMGS):
        for t in range(TOKENS):
            take[i * WPAD + t, t * IMGS + i] = 1
    return take


def dot(a, b):
    return lax.dot_general(a, b, (((1,), (0,)), ((), ())), preferred_element_type=f32)


def dot_nt(a, b):
    return lax.dot_general(a, b, (((1,), (1,)), ((), ())), preferred_element_type=f32)


def dot_tn(a, b):
    return lax.dot_general(a, b, (((0,), (0,)), ((), ())), preferred_element_type=f32)


def normed(x):
    centred = x - jnp.mean(x, axis=-1, keepdims=True)
    rstd = lax.rsqrt(jnp.mean(centred * centred, axis=-1, keepdims=True) + EPSILON)
    return centred * rstd, rstd


def norm_back(grad, gain, hat, rstd):
    g = grad * gain
    mean_g = jnp.mean(g, axis=-1, keepdims=True)
    mean_gh = jnp.mean(g * hat, axis=-1, keepdims=True)
    return rstd * (g - mean_g - hat * mean_gh)


def spread_heads(block, head_mask):
    return jnp.concatenate([block] * PACK, axis=0) * head_mask


def gather_heads(result):
    lane = lax.broadcasted_iota(jnp.int32, (WPAD, GCOLS), 1) // HEAD
    parts = [result[h * WPAD : (h + 1) * WPAD] for h in range(PACK)]
    out = parts[PACK - 1]
    for h in range(PACK - 2, -1, -1):
        out = jnp.where(lane == h, parts[h], out)
    return out


def token_places(place):
    row0 = (place // CELLS) * WIN + SHIFT
    col0 = (place % CELLS) * WIN + SHIFT
    for i in range(WIN):
        r = row0 + i
        r = jnp.where(r >= SIDE, r - SIDE, r)
        for j in range(WIN):
            c = col0 + j
            yield (i * WIN + j) * IMGS, r, jnp.where(c >= SIDE, c - SIDE, c)


def load_window(rows, ref, place):
    for at, r, c in token_places(place):
        rows[at : at + IMGS] = ref[r, c].astype(f32)
    return rows[...]


def store_window(ref, value, place):
    for at, r, c in token_places(place):
        ref[r, c] = value[at : at + IMGS].astype(bf16)


def join_rows(full, own_ref, other_ref):
    half = full.shape[0] // 2
    first = lax.axis_index("shard") == 0

    @pl.when(first)
    def _():
        full[0:half] = own_ref[...]
        full[half:] = other_ref[...]

    @pl.when(jnp.logical_not(first))
    def _():
        full[0:half] = other_ref[...]
        full[half:] = own_ref[...]


def join_vectors(vec, own_ref, other_ref):
    first = lax.axis_index("shard") == 0
    own, other = own_ref[...].astype(f32), other_ref[...].astype(f32)
    vec[:, 0 : D // 2] = jnp.where(first, own, other)
    vec[:, D // 2 :] = jnp.where(first, other, own)


G1, B1, QB, VB, PB, G2, B2, F2B, FB = range(9)
VROWS = 12


def forward_kernel(
    count_ref, img_ref, og_ref, take_ref, put_ref, qw0_ref, qw1_ref, pw0_ref, pw1_ref,
    vec0_ref, vec1_ref, pos_ref, mask_ref, hm_ref,
    qkv_out, prob_out, h1_out, att_out, mid_out, h2_out, cot_out, cotsum_out,
    rows_in, att, qkvw_ref, pw_ref, vec,
):
    place = pl.program_id(0)

    @pl.when(place == 0)
    def _():
        cotsum_out[...] = jnp.zeros_like(cotsum_out)
        join_rows(qkvw_ref, qw0_ref, qw1_ref)
        join_rows(pw_ref, pw0_ref, pw1_ref)
        join_vectors(vec, vec0_ref, vec1_ref)

    def row(at):
        return vec[at : at + 1]

    image = lax.broadcasted_iota(jnp.int32, (DROWS, D), 0) % IMGS
    cot = jnp.where(image < count_ref[0], load_window(rows_in, og_ref, place), 0.0)
    cot_out[...] = cot.astype(bf16)
    cotsum_out[...] += jnp.sum(cot, axis=0, keepdims=True)

    x = load_window(rows_in, img_ref, place)
    hat, _ = normed(x)
    h1 = (hat * row(G1) + row(B1)).astype(bf16)
    h1_out[...] = h1
    tiles = dot(take_ref[...], h1).astype(bf16)
    qkv_out[:, 0:D] = (dot(tiles, qkvw_ref[:, 0:D]) + row(QB)).astype(bf16)
    qkv_out[:, D : 2 * D] = dot(tiles, qkvw_ref[:, D : 2 * D]).astype(bf16)
    qkv_out[:, 2 * D : 3 * D] = (dot(tiles, qkvw_ref[:, 2 * D : 3 * D]) + row(VB)).astype(bf16)
    head_mask = hm_ref[...]
    units = [(i, g) for g in range(GROUPS) for i in range(IMGS)]
    for at in range(0, len(units), BATCH):
        batch = units[at : at + BATCH]
        rows = [slice(i * WPAD, (i + 1) * WPAD) for i, _ in batch]
        cols = [slice(g * GCOLS, (g + 1) * GCOLS) for _, g in batch]
        wide = [spread_heads(qkv_out[r, c], head_mask) for r, c in zip(rows, cols)]
        keys = [qkv_out[r, D + c.start : D + c.stop] for r, c in zip(rows, cols)]
        s = [dot_nt(k, q)[:KEEP] for k, q in zip(keys, wide)]
        s = [v * SCALE + pos_ref[g] + mask_ref[...] for v, (_, g) in zip(s, batch)]
        e = [jnp.exp(v - jnp.max(v, axis=0, keepdims=True)) for v in s]
        p = [v / jnp.sum(v, axis=0, keepdims=True) for v in e]
        zero = jnp.zeros((WPAD - KEEP, LANES), f32)
        p = [jnp.concatenate([v, zero], axis=0).astype(bf16) for v in p]
        for v, (i, g) in zip(p, batch):
            prob_out[g, i] = v
        values = [qkv_out[r, 2 * D + c.start : 2 * D + c.stop] for r, c in zip(rows, cols)]
        found = [dot_tn(v, w) for v, w in zip(p, values)]
        for r, c, v in zip(rows, cols, found):
            att[r, c] = gather_heads(v).astype(bf16)
    a = dot(put_ref[...], att[...]).astype(bf16)
    att_out[...] = a
    middle = x + (dot(a, pw_ref[...]) + row(PB))
    mid_out[...] = middle
    hat2, _ = normed(middle)
    h2_out[...] = (hat2 * row(G2) + row(B2)).astype(bf16)


def ffn_kernel(which, last, *refs):
    refs = list(refs)
    h2_ref, cot_ref, f10_ref, f11_ref, f20_ref, f21_ref, vec0_ref, vec1_ref = refs[:8]
    refs = refs[8:]
    if last:
        oin_ref, din_ref, mid_ref = refs[:3]
        refs = refs[3:]
    send, keep, bias_out, out_ref, dh2_ref = refs[:5]
    acc1, acc2, oacc, dacc, f1_ref, f2_ref, vec, fbias = refs[5:]
    j, c = pl.program_id(0), pl.program_id(1)

    @pl.when(c == 0)
    def _():
        mine = lax.axis_index("shard") == j
        join_rows(f1_ref, f10_ref, f11_ref)
        join_vectors(vec, vec0_ref, vec1_ref)

        def owner_parts(f2, vectors):
            f2_ref[...] = f2[...]
            for b in range(BLOCK // (D // 2)):
                at = FB + which * (BLOCK // (D // 2)) + b
                fbias[:, b * D // 2 : (b + 1) * D // 2] = vectors[at : at + 1].astype(f32)

        @pl.when(mine)
        def _():
            owner_parts(f20_ref, vec0_ref)

        @pl.when(jnp.logical_not(mine))
        def _():
            owner_parts(f21_ref, vec1_ref)

    h2 = h2_ref[...]
    cot = cot_ref[...]
    hidden = dot(h2, f1_ref[...]) + fbias[...]
    dact = dot_nt(cot, f2_ref[...])
    bell = jnp.exp(hidden * hidden * -0.5)
    base = 1.0 + jnp.abs(hidden) * (0.3275911 * 0.5**0.5)
    t = pl.reciprocal(base, approx=True)
    t = t * (2.0 - base * t)
    half = t * (
        0.127414796
        + t * (-0.142248368 + t * (0.7107068705 + t * (-0.7265760135 + t * 0.5307027145)))
    )
    half = half * bell
    phi = jnp.where(hidden > 0, 1.0 - half, half)
    act = (hidden * phi).astype(bf16)
    dhid = dact * (phi + hidden * bell * 0.3989422804014327)
    dhid_low = dhid.astype(bf16)

    g2 = dot_tn(act, cot)
    g1 = dot_tn(h2, dhid_low)
    fb = jnp.sum(dhid, axis=0, keepdims=True)
    o = dot(act, f2_ref[...])
    d = dot_nt(dhid_low, f1_ref[...])

    acc1[...] = jnp.where(c == 0, 0.0, acc1[...]) + g1
    acc2[...] = jnp.where(c == 0, 0.0, acc2[...]) + g2
    bias_out[0] = jnp.where(c == 0, 0.0, bias_out[0]) + fb
    o = jnp.where(j == 0, 0.0, oacc[c]) + o
    d = jnp.where(j == 0, 0.0, dacc[c]) + d
    oacc[c] = o
    dacc[c] = d
    if last:
        dh2_ref[...] = d + din_ref[...]
        store_window(out_ref, mid_ref[...] + (o + oin_ref[...]) + vec[F2B : F2B + 1], c)
    else:
        dh2_ref[...] = d
        out_ref[...] = o

    half_rows = D // 2

    @pl.when(c == pl.num_programs(1) - 1)
    def _():
        mine = lax.axis_index("shard")

        def hand_out(owner, at, value):
            @pl.when(owner == mine)
            def _():
                keep[at] = value

            @pl.when(owner != mine)
            def _():
                send[at] = value

        hand_out(j, slice(0, BLOCK), acc2[...].astype(bf16))
        place = pl.ds(pl.multiple_of(BLOCK + j * half_rows, half_rows), half_rows)
        hand_out(0, place, acc1[0:half_rows].astype(bf16))
        hand_out(1, place, acc1[half_rows:D].astype(bf16))


def middle_kernel(
    cot_ref, dh2_ref, mid_ref, att_ref, take_ref, pw0_ref, pw1_ref, vec0_ref, vec1_ref,
    dmid_out, dwin_out, grads, small, gp, pw_ref, vec,
):
    place = pl.program_id(0)

    @pl.when(place == 0)
    def _():
        small[...] = jnp.zeros_like(small)
        gp[...] = jnp.zeros_like(gp)
        join_rows(pw_ref, pw0_ref, pw1_ref)
        join_vectors(vec, vec0_ref, vec1_ref)

    hat2, rstd2 = normed(mid_ref[...])
    dh2 = dh2_ref[...]
    small[0:1] += jnp.sum(dh2 * hat2, axis=0, keepdims=True)
    small[1:2] += jnp.sum(dh2, axis=0, keepdims=True)
    dmid = cot_ref[...].astype(f32) + norm_back(dh2, vec[G2 : G2 + 1], hat2, rstd2)
    small[2:3] += jnp.sum(dmid, axis=0, keepdims=True)
    dmid_out[...] = dmid
    dbr = dmid.astype(bf16)
    gp[...] += dot_tn(att_ref[...], dbr)
    datt = dot_nt(dbr, pw_ref[...]).astype(bf16)
    dwin_out[...] = dot(take_ref[...], datt).astype(bf16)

    @pl.when(place == pl.num_programs(0) - 1)
    def _():
        half = D // 2
        for o in range(2):
            for b in range(2):
                grads[o, b * half : (b + 1) * half] = gp[
                    o * half : (o + 1) * half, b * half : (b + 1) * half
                ].astype(bf16)


def heads_kernel(
    q_ref, k_ref, v_ref, prob_ref, dwin_ref, h1_ref, put_ref, hm_ref,
    dm_out, grads, small, bias_out, dmix, gq,
):
    place = pl.program_id(0)

    @pl.when(place == 0)
    def _():
        small[...] = jnp.zeros_like(small)
        bias_out[...] = jnp.zeros_like(bias_out)
        gq[...] = jnp.zeros_like(gq)

    head_mask = hm_ref[...]
    units = [(i, g) for g in range(PART) for i in range(IMGS)]
    zero = jnp.zeros((WPAD - KEEP, LANES), f32)
    for at in range(0, len(units), BATCH):
        batch = units[at : at + BATCH]
        rows = [slice(i * WPAD, (i + 1) * WPAD) for i, _ in batch]
        cols = [slice(g * GCOLS, (g + 1) * GCOLS) for _, g in batch]
        wide = [spread_heads(dwin_ref[r, c], head_mask) for r, c in zip(rows, cols)]
        dp = [dot_nt(v_ref[r, c], da)[:KEEP] for r, c, da in zip(rows, cols, wide)]
        low = [prob_ref[g, i] for i, g in batch]
        dv = [dot(p, da) for p, da in zip(low, wide)]
        p = [v.astype(f32)[:KEEP] for v in low]
        inner = [jnp.sum(x * y, axis=0, keepdims=True) for x, y in zip(dp, p)]
        ds = [(y * (x - n)).astype(bf16).astype(f32) for x, y, n in zip(dp, p, inner)]
        for v, (_, g) in zip(ds, batch):
            bias_out[g] += v
        ds = [jnp.concatenate([v, zero], axis=0).astype(bf16) for v in ds]
        dq = [dot_tn(v, k_ref[r, c]) for v, r, c in zip(ds, rows, cols)]
        queries = [spread_heads(q_ref[r, c], head_mask) for r, c in zip(rows, cols)]
        dk = [dot(v, q) for v, q in zip(ds, queries)]
        for r, c, x, y, w in zip(rows, cols, dq, dk, dv):
            dmix[r, c] = (gather_heads(x) * SCALE).astype(bf16)
            dmix[r, PCOLS + c.start : PCOLS + c.stop] = (y * SCALE).astype(bf16)
            dmix[r, 2 * PCOLS + c.start : 2 * PCOLS + c.stop] = w.astype(bf16)
    small[0:1] += jnp.sum(dmix[:, 0:PCOLS].astype(f32), axis=0, keepdims=True)
    small[1:2] += jnp.sum(dmix[:, 2 * PCOLS : 3 * PCOLS].astype(f32), axis=0, keepdims=True)
    dm = dot(put_ref[...], dmix[...]).astype(bf16)
    dm_out[...] = dm
    gq[...] += dot_tn(h1_ref[...], dm)

    @pl.when(place == pl.num_programs(0) - 1)
    def _():
        half = D // 2
        for o in range(2):
            for b in range(3):
                grads[o, b * half : (b + 1) * half] = gq[
                    o * half : (o + 1) * half, b * PCOLS : (b + 1) * PCOLS
                ].astype(bf16)


def final_kernel(
    img_ref, dmid_ref, dm0_ref, dm1_ref, qw0_ref, qw1_ref, vec0_ref, vec1_ref,
    out_ref, small, rows_in, qkvw_ref, vec,
):
    place = pl.program_id(0)

    @pl.when(place == 0)
    def _():
        small[...] = jnp.zeros_like(small)
        join_rows(qkvw_ref, qw0_ref, qw1_ref)
        join_vectors(vec, vec0_ref, vec1_ref)

    dh1 = None
    for part, ref in enumerate((dm0_ref, dm1_ref)):
        for b in range(3):
            at = b * D + part * PCOLS
            term = dot_nt(ref[:, b * PCOLS : (b + 1) * PCOLS], qkvw_ref[:, at : at + PCOLS])
            dh1 = term if dh1 is None else dh1 + term
    hat1, rstd1 = normed(load_window(rows_in, img_ref, place))
    small[0:1] += jnp.sum(dh1 * hat1, axis=0, keepdims=True)
    small[1:2] += jnp.sum(dh1, axis=0, keepdims=True)
    store_window(out_ref, dmid_ref[...] + norm_back(dh1, vec[G1 : G1 + 1], hat1, rstd1), place)


def far(value):
    return pltpu.with_memory_space_constraint(value, pltpu.HBM)


def all_far(values):
    return [far(value) for value in values]


def whole(shape):
    return pl.BlockSpec(shape, lambda *_: (0,) * len(shape))


def by_place(*dims):
    return pl.BlockSpec((None,) + dims, lambda i: (i,) + (0,) * len(dims))


def params(axes, flops, size):
    return dict(
        compiler_params=pltpu.CompilerParams(
            dimension_semantics=("arbitrary",) * axes, vmem_limit_bytes=24 * 1024 * 1024
        ),
        cost_estimate=pl.CostEstimate(flops=int(flops), bytes_accessed=int(size), transcendentals=0),
    )


IMAGE = (SIDE, SIDE, IMGS, D)


def dense(kind, cols=D):
    return jax.ShapeDtypeStruct((WINDOWS, DROWS, cols), kind)


VECTORS = pltpu.VMEM((VROWS, D), f32)


def run_forward(images, out_grad, count, take, put, qkvw, pw, vec, pos, mask, hm):
    drow = by_place(DROWS, D)
    pair = [whole(qkvw[0].shape)] * 2 + [whole(pw[0].shape)] * 2 + [whole(vec[0].shape)] * 2
    return pl.pallas_call(
        forward_kernel,
        grid=(WINDOWS,),
        in_specs=[
            pl.BlockSpec(memory_space=pltpu.SMEM), whole(IMAGE), whole(IMAGE),
            whole(take.shape), whole(put.shape), *pair,
            whole(pos.shape), by_place(KEEP, LANES), whole(hm.shape),
        ],
        out_specs=[
            by_place(WROWS, 3 * D), by_place(GROUPS, IMGS, WPAD, LANES),
            drow, drow, drow, drow, drow, whole((1, D)),
        ],
        out_shape=[
            pltpu.HBM((WINDOWS, WROWS, 3 * D), bf16),
            pltpu.HBM((WINDOWS, GROUPS, IMGS, WPAD, LANES), bf16),
            pltpu.HBM((WINDOWS, DROWS, D), bf16), pltpu.HBM((WINDOWS, DROWS, D), bf16),
            pltpu.HBM((WINDOWS, DROWS, D), f32), dense(bf16), dense(bf16),
            jax.ShapeDtypeStruct((1, D), f32),
        ],
        scratch_shapes=[
            pltpu.VMEM((DROWS, D), f32), pltpu.VMEM((WROWS, D), bf16),
            pltpu.VMEM((D, 3 * D), bf16), pltpu.VMEM((D, D), bf16), VECTORS,
        ],
        name="forward_attention",
        **params(1, 9e9, 25e6),
    )(count, *all_far([images, out_grad, take, put, *qkvw, *pw, *vec, pos, mask, hm]))


def run_ffn(which, h2, cot, fc1, fc2, vec, finish=None):
    last = finish is not None
    chunk = pl.BlockSpec((None, DROWS, D), lambda j, c: (c, 0, 0))
    late = pl.BlockSpec((None, DROWS, D), lambda j, c: (c * j, 0, 0))
    f1 = pl.BlockSpec((D // 2, BLOCK), lambda j, c: (0, 2 * j + which))
    f2 = pl.BlockSpec((BLOCK, D), lambda j, c: (which, 0))
    vecs = whole(vec[0].shape)
    in_specs = [chunk, chunk, f1, f1, f2, f2, vecs, vecs]
    args = [h2, cot, *all_far([*fc1, *fc2, *vec])]
    out, out_spec = pltpu.HBM((WINDOWS, DROWS, D), f32), late
    if last:
        in_specs += [late, late, late]
        args += all_far(finish)
        out, out_spec = jax.ShapeDtypeStruct(IMAGE, bf16), whole(IMAGE)
    return pl.pallas_call(
        functools.partial(ffn_kernel, which, last),
        grid=(2, WINDOWS),
        in_specs=in_specs,
        out_specs=[
            *[whole((2 * BLOCK, D))] * 2, pl.BlockSpec((1, 1, BLOCK), lambda j, c: (j, 0, 0)),
            out_spec, late,
        ],
        out_shape=[
            *[jax.ShapeDtypeStruct((2 * BLOCK, D), bf16)] * 2,
            jax.ShapeDtypeStruct((2, 1, BLOCK), f32), out,
            pltpu.HBM((WINDOWS, DROWS, D), f32),
        ],
        scratch_shapes=[
            pltpu.VMEM((D, BLOCK), f32), pltpu.VMEM((BLOCK, D), f32),
            pltpu.VMEM((WINDOWS, DROWS, D), f32), pltpu.VMEM((WINDOWS, DROWS, D), f32),
            pltpu.VMEM((D, BLOCK), bf16), pltpu.VMEM((BLOCK, D), bf16), VECTORS,
            pltpu.VMEM((1, BLOCK), f32),
        ],
        name="ffn",
        **params(2, 2 * 12 * WINDOWS * DROWS * D * BLOCK, 20e6),
    )(*args)


def run_middle(cot, dh2, mid, att, take, pw, vec):
    drow = by_place(DROWS, D)
    return pl.pallas_call(
        middle_kernel,
        grid=(WINDOWS,),
        in_specs=[
            drow, drow, drow, drow, whole(take.shape), *[whole(pw[0].shape)] * 2,
            *[whole(vec[0].shape)] * 2,
        ],
        out_specs=[drow, by_place(WROWS, D), whole((2, D, D // 2)), whole((8, D))],
        out_shape=[
            dense(f32), jax.ShapeDtypeStruct((WINDOWS, WROWS, D), bf16),
            jax.ShapeDtypeStruct((2, D, D // 2), bf16), jax.ShapeDtypeStruct((8, D), f32),
        ],
        scratch_shapes=[pltpu.VMEM((D, D), f32), pltpu.VMEM((D, D), bf16), VECTORS],
        name="middle_backward",
        **params(1, 3e9, 10e6),
    )(*all_far([cot, dh2, mid, att, take, *pw, *vec]))


def run_heads(part, qkv, prob, dwin, h1, put, hm):
    def columns(at):
        return pl.BlockSpec((None, WROWS, PCOLS), lambda i: (i, 0, at))

    rows = 3 * (D // 2)
    return pl.pallas_call(
        heads_kernel,
        grid=(WINDOWS,),
        in_specs=[
            columns(part), columns(SPLIT + part), columns(2 * SPLIT + part),
            pl.BlockSpec((None, PART, IMGS, WPAD, LANES), lambda i: (i, part, 0, 0, 0)),
            columns(part), by_place(DROWS, D), whole(put.shape), whole(hm.shape),
        ],
        out_specs=[
            by_place(DROWS, 3 * PCOLS), whole((2, rows, D // 2)), whole((8, PCOLS)),
            whole((PART, KEEP, LANES)),
        ],
        out_shape=[
            pltpu.HBM((WINDOWS, DROWS, 3 * PCOLS), bf16),
            jax.ShapeDtypeStruct((2, rows, D // 2), bf16),
            jax.ShapeDtypeStruct((8, PCOLS), f32),
            jax.ShapeDtypeStruct((PART, KEEP, LANES), f32),
        ],
        scratch_shapes=[
            pltpu.VMEM((WROWS, 3 * PCOLS), bf16), pltpu.VMEM((D, 3 * PCOLS), f32),
        ],
        name="attention_backward",
        **params(1, 4e9, 10e6),
    )(*all_far([qkv, qkv, qkv, prob]), dwin, *all_far([h1, put, hm]))


def run_final(images, dmid, dm0, dm1, qkvw, vec):
    return pl.pallas_call(
        final_kernel,
        grid=(WINDOWS,),
        in_specs=[
            whole(IMAGE), by_place(DROWS, D), by_place(DROWS, 3 * PCOLS),
            by_place(DROWS, 3 * PCOLS), *[whole(qkvw[0].shape)] * 2, *[whole(vec[0].shape)] * 2,
        ],
        out_specs=[whole(IMAGE), whole((8, D))],
        out_shape=[jax.ShapeDtypeStruct(IMAGE, bf16), jax.ShapeDtypeStruct((8, D), f32)],
        scratch_shapes=[pltpu.VMEM((DROWS, D), f32), pltpu.VMEM((D, 3 * D), bf16), VECTORS],
        name="final_backward",
        **params(1, 3e9, 10e6),
    )(far(images), dmid, *all_far([dm0, dm1, *qkvw, *vec]))


def digits_of(n):
    digits, stride = [], 1
    while n > 1:
        base = 4 if n % 4 == 0 else 2
        digits.append((base, stride))
        stride *= base
        n //= base
    return digits


def make_shards(replicas):
    axes = ("replica", "shard")
    core_pairs = [(r * 2 + s, r * 2 + 1 - s) for r in range(replicas) for s in range(2)]
    digits = digits_of(replicas)

    def across(value):
        return lax.ppermute(value, axes, core_pairs)

    def partner(value, k, stride):
        pairs = [(r * 2 + s, (r ^ (k * stride)) * 2 + s) for r in range(replicas) for s in range(2)]
        return lax.ppermute(value, axes, pairs)

    def place(base, stride):
        return (lax.axis_index("replica") // stride) % base

    def pick(value, index):
        return lax.dynamic_index_in_dim(value, index, 0, keepdims=False)

    def in_order(parts, mine):
        base = len(parts)
        laid = []
        for at in range(base):
            value = parts[at]
            for c in range(1, base):
                value = jnp.where(mine == c, parts[at ^ c], value)
            laid.append(value)
        return jnp.stack(laid)

    def both_halves(value):
        other = across(value)
        first = lax.axis_index("shard") == 0
        return jnp.where(first, value, other), jnp.where(first, other, value)

    def tie(*values):
        return lax.optimization_barrier(values)

    def core_halves(parts):
        s = lax.axis_index("shard")
        return [
            jnp.concatenate([pick(part, at) for part in parts], axis=0) for at in (1 - s, s)
        ]

    def added(*values):
        total = values[0].astype(f32)
        for value in values[1:]:
            total = total + value.astype(f32)
        return total.astype(bf16)

    def split_sends(buf, base, stride):
        mine = place(base, stride)
        view = buf.reshape(base, buf.shape[0] // base, buf.shape[1])
        return pick(view, mine), [pick(view, mine ^ k) for k in range(1, base)]

    def swap(sends, stride):
        return [partner(value, k + 1, stride) for k, value in enumerate(sends)]

    def two_parts(value):
        top = lax.reduce_precision(value, 8, 7)
        return jnp.concatenate([top.astype(bf16), (value - top).astype(bf16)], axis=0)

    def one_part(rows):
        half = rows.shape[0] // 2
        return rows[:half].astype(f32) + rows[half:].astype(f32)

    def shards(
        images, out_grad, image_counts, regions, relative_index,
        norm1_gain, norm1_bias, qkv_weight, query_bias, value_bias, bias_table,
        proj_weight, proj_bias, norm2_gain, norm2_bias, fc1_weight, fc1_bias, fc2_weight, fc2_bias,
    ):
        shard = lax.axis_index("shard")
        half = D // 2
        images = images.transpose(1, 2, 0, 3)
        out_grad = out_grad.transpose(1, 2, 0, 3)
        qkvw = (qkv_weight, across(qkv_weight))
        vectors = [
            norm1_gain, norm1_bias, query_bias, value_bias,
            proj_bias, norm2_gain, norm2_bias, fc2_bias,
        ] + [fc1_bias[i * half : (i + 1) * half] for i in range(VROWS - FB)]
        at_row = lax.broadcasted_iota(jnp.int32, (VROWS, half), 0)
        packed = jnp.zeros((VROWS, half), bf16)
        for i, value in enumerate(vectors):
            packed = jnp.where(at_row == i, value[None, :], packed)
        vec = (packed, across(packed))
        table = jnp.concatenate(both_halves(bias_table.T), axis=0)
        pw = (proj_weight, across(proj_weight))
        fc1 = (fc1_weight, across(fc1_weight))
        fc2 = (fc2_weight, across(fc2_weight))

        index = jnp.pad(
            relative_index.T, ((0, KEEP - TOKENS), (0, WPAD - TOKENS)), constant_values=-1
        )
        onehot = (
            index.reshape(1, -1) == jnp.arange(TABLE, dtype=jnp.int32)[:, None]
        ).astype(bf16)
        pos = dot(table, onehot).reshape(GROUPS, PACK, KEEP, WPAD)
        pos = pos.transpose(0, 2, 1, 3).reshape(GROUPS, KEEP, LANES)
        labels = regions.reshape(CELLS, WIN, CELLS, WIN).transpose(0, 2, 1, 3)
        labels = labels.reshape(WINDOWS, TOKENS)
        differ = labels[:, :, None] != labels[:, None, :]
        mask = jnp.where(differ, MASK_FILL, 0.0).astype(f32)
        mask = jnp.pad(mask, ((0, 0), (0, 0), (0, WPAD - TOKENS)))
        mask = jnp.pad(mask, ((0, 0), (0, KEEP - TOKENS), (0, 0)), constant_values=PAD_FILL)
        mask = jnp.tile(mask, (1, 1, PACK))

        take_np = window_places()
        take = jnp.asarray(take_np, bf16)
        put = jnp.asarray(take_np.T, bf16)
        hm = jnp.asarray(
            (np.arange(LANES)[:, None] // WPAD) == (np.arange(GCOLS)[None, :] // HEAD), bf16
        )

        qkv, prob, h1, att, mid, h2, cot, cotsum = run_forward(
            images, out_grad, image_counts, take, put, qkvw, pw, vec, pos, mask, hm
        )
        near, wide = digits[0], digits[-1]

        def inner(buf):
            for base, stride in digits[1:-1]:
                kept, sends = split_sends(buf, base, stride)
                buf = added(kept, *swap(sends, stride))
            return buf

        def back(buf, gots, base, stride):
            return in_order([buf] + gots, place(base, stride)).reshape(-1, buf.shape[1])

        def inner_back(buf):
            for base, stride in reversed(digits[1:-1]):
                buf = back(buf, swap([buf] * (base - 1), stride), base, stride)
            return buf

        def spread(buf, base, stride):
            return swap([buf] * (base - 1), stride)

        send, keep, fbias_a, oacc, dacc = run_ffn(0, h2, cot, fc1, fc2, vec)
        kept_a, sends_a = split_sends(added(keep, across(send)), *near)
        kept_a, sends_a, h2 = tie(kept_a, sends_a, h2)
        gots_a = swap(sends_a, near[1])

        send, keep, fbias_b, output, dh2 = run_ffn(
            1, h2, cot, fc1, fc2, vec, (oacc, dacc, mid)
        )
        kept_a, gots_a, send, dh2 = tie(kept_a, gots_a, send, dh2)
        got = across(send)
        kept_a, sends_a = split_sends(inner(added(kept_a, *gots_a)), *wide)
        kept_a, sends_a, dh2 = tie(kept_a, sends_a, dh2)
        gots_a = swap(sends_a, wide[1])

        dmid, dwin, gp, small_mid = run_middle(cot, dh2, mid, att, take, pw, vec)
        kept_a, gots_a, got, dwin = tie(kept_a, gots_a, got, dwin)
        kept_b, sends_b = split_sends(added(keep, got), *near)
        buf_a = added(kept_a, *gots_a)
        buf_a, kept_b, sends_b, dwin = tie(buf_a, kept_b, sends_b, dwin)
        gots_a = spread(buf_a, *wide)
        gots_b = swap(sends_b, near[1])

        dm0, grads_c, small_c, bias_c = run_heads(0, qkv, prob, dwin, h1, put, hm)
        kept_b, gots_b, dm0, dwin = tie(kept_b, gots_b, dm0, dwin)
        kept_b, sends_b = split_sends(inner(added(kept_b, *gots_b)), *wide)
        kept_b, sends_b, dwin = tie(kept_b, sends_b, dwin)
        gots_b = swap(sends_b, wide[1])

        dm1, grads_d, small_d, bias_d = run_heads(1, qkv, prob, dwin, h1, put, hm)
        send, keep = core_halves([grads_c, gp, grads_d])
        send, dm1, buf_a, gots_a = tie(send, dm1, buf_a, gots_a)
        buf_a = inner_back(back(buf_a, gots_a, *wide))
        gots_a = spread(buf_a, *near)
        kept, sends = split_sends(added(keep, across(send)), *near)
        kept, sends, dm1 = tie(kept, sends, dm1)
        gots = swap(sends, near[1])

        grad_images, small_end = run_final(images, dmid, dm0, dm1, qkvw, vec)
        kept, gots, buf_a, gots_a, kept_b, gots_b, bias_c, bias_d, small_end = tie(
            kept, gots, buf_a, gots_a, kept_b, gots_b, bias_c, bias_d, small_end
        )
        bias_sum = jnp.concatenate([bias_c, bias_d], axis=0)
        by_head = bias_sum.reshape(GROUPS, KEEP, PACK, WPAD).transpose(0, 2, 1, 3)
        table_grad = lax.dot_general(
            by_head.reshape(HEADS, -1), onehot.astype(f32), (((1,), (1,)), ((), ())),
            precision=HIGH, preferred_element_type=f32,
        )
        table_rows = jnp.pad(table_grad, ((0, 0), (0, half - TABLE)))
        fbias = [fbias_a[0], fbias_b[0], fbias_a[1], fbias_b[1]]
        rows = jnp.concatenate([small_end[0:2], small_mid[0:3], cotsum, *fbias], axis=0)
        small = jnp.concatenate(
            [rows[:, :half], rows[:, half:], small_c[0:2], small_d[0:2], table_rows], axis=0
        )

        buf = added(kept, *gots)
        for base, stride in digits[1:]:
            kept, sends = split_sends(buf, base, stride)
            extra = two_parts(small)
            cut = kept.shape[0]
            sends = [jnp.concatenate([value, extra], axis=0) for value in sends]
            sends, kept_b, gots_b, buf_a, gots_a = tie(sends, kept_b, gots_b, buf_a, gots_a)
            gots = swap(sends, stride)
            buf = added(kept, *[value[:cut] for value in gots])
            for value in gots:
                small = small + one_part(value[cut:])

        buf_a = back(buf_a, gots_a, *near)
        buf_b = added(kept_b, *gots_b)
        buf_b = inner_back(back(buf_b, spread(buf_b, *wide), *wide))
        buf_b = back(buf_b, spread(buf_b, *near), *near)
        for base, stride in reversed(digits[1:]):
            buf = back(buf, swap([buf] * (base - 1), stride), base, stride)
        base, stride = digits[0]
        cut = buf.shape[0]
        extra = two_parts(small)
        gots = swap([jnp.concatenate([buf, extra], axis=0)] * (base - 1), stride)
        buf = back(buf, [value[:cut] for value in gots], base, stride)
        for value in gots:
            small = small + one_part(value[cut:])
        small = small + across(small)
        sum_a, sum_b, sum_c = buf_a.astype(f32), buf_b.astype(f32), buf.astype(f32)

        n = 2 + 3 + 1 + 4
        mine = lax.dynamic_slice(small, (shard * n, 0), (n, half))
        sides = small[2 * n : 2 * n + 4]
        query_sum, value_sum = [
            lax.dynamic_index_in_dim(sides[i::2], shard, 0, keepdims=False) for i in range(2)
        ]
        own_table = lax.dynamic_slice(
            small, (2 * n + 4 + shard * (HEADS // 2), 0), (HEADS // 2, half)
        )[:, :TABLE].T
        fsum = small[: 2 * n].reshape(2, n, half)[:, 6:]
        own_fb = lax.dynamic_slice(fsum, (0, 2 * shard, 0), (2, 2, half))
        own_fb = own_fb.transpose(1, 0, 2).reshape(-1)
        grad_fc2 = jnp.concatenate([sum_a[:BLOCK], sum_b[:BLOCK]], axis=0)
        grad_fc1 = jnp.concatenate(
            [sum_a[BLOCK : BLOCK + half], sum_b[BLOCK : BLOCK + half],
             sum_a[BLOCK + half :], sum_b[BLOCK + half :]], axis=1,
        )
        start = 3 * half + D
        grad_qkv = jnp.concatenate(
            [sum_c[at + b * half : at + (b + 1) * half] for b in range(3) for at in (0, start)],
            axis=1,
        )
        grad_proj = jnp.concatenate(
            [sum_c[3 * half : 4 * half], sum_c[4 * half : 5 * half]], axis=1
        )
        return (
            output.transpose(2, 0, 1, 3), grad_images.transpose(2, 0, 1, 3),
            mine[0], mine[1], grad_qkv, query_sum, value_sum, own_table,
            grad_proj, mine[4], mine[2], mine[3], grad_fc1, own_fb, grad_fc2, mine[5],
        )

    return shards


def solution(mesh):
    return jax.shard_map(
        make_shards(mesh.shape["replica"]),
        mesh=mesh,
        in_specs=(
            P(("replica", "shard"), None, None, None),
            P(("replica", "shard"), None, None, None),
            P(("replica", "shard")),
            P(),
            P(),
            P("shard"),
            P("shard"),
            P("shard", None),
            P("shard"),
            P("shard"),
            P(None, "shard"),
            P("shard", None),
            P("shard"),
            P("shard"),
            P("shard"),
            P("shard", None),
            P("shard"),
            P("shard", None),
            P("shard"),
        ),
        out_specs=(
            P(("replica", "shard"), None, None, None),
            P(("replica", "shard"), None, None, None),
            P("shard"),
            P("shard"),
            P("shard", None),
            P("shard"),
            P("shard"),
            P(None, "shard"),
            P("shard", None),
            P("shard"),
            P("shard"),
            P("shard"),
            P("shard", None),
            P("shard"),
            P("shard", None),
            P("shard"),
        ),
        check_vma=False,
    )
```
